32 devices in a mesh: list: 4 (over y, core), shard: 8 (over z, x).
Axes of the slice: x: 2, y: 2, z: 4, core: 2. Of those that a mesh axis runs over, the one named last changes fastest.
Arguments:
- embeddings: bfloat16 [65536, 768], P(('list', 'shard')), may hold values from -6 to 6
- list_ids: int32 [65536, 1], P(('list', 'shard')), may hold values from 0 to 7; in each aligned block of 2048 rows (0 to 2047, 2048 to 4095, ...) at most 256 rows name the same one
- centroids: bfloat16 [8, 1024, 768], P('list'), may hold values from -6 to 6
Outputs:
- new_centroids: float32 [8, 1024, 768], P('list', 'shard')
The draws below stay inside these ranges and needn't reach their ends.
Inputs may be any that keep to these rules, and one draw needn't show every extreme that they name: `list_ids`: within each device's 2048 rows no coarse list is named by more than 256 rows, a bound that some block reaches.
All inputs are finite; a program needn't handle non-finite values.
Results may differ from the reference program's by a relative error of at most 0.0014.
Values may be sent and summed in bfloat16 or wider, within the bound.
A program may use at most 64 MiB of HBM per device.

```python
import math
import jax
import jax.numpy as jnp
import numpy as np
from jax import lax

D = 768
FINE = 1024
R_DEV = 2048
CAP = 256
LISTS = 8
ROWS = 65536
N_LIST = 4
N_SHARD = 8


def block_scale(own_key, extent, pieces, low, largest):
    loudness = 1.0
    for axis_at, shards_of in pieces:
        heights = jax.random.uniform(jax.random.fold_in(jax.random.fold_in(own_key, 6), axis_at), (shards_of,), jnp.float32, low / len(pieces), largest / len(pieces))
        loudness = loudness * jnp.repeat(jnp.exp(heights), extent[axis_at] // shards_of).reshape((-1,) + (1,) * (len(extent) - 1 - axis_at))
    return loudness


def routed_block(rng, own, number, rows, count, top, bound, skew):
    ranking = jax.random.permutation(rng, count)
    packed, usual = load_shares(count, rows * top, bound, skew, True), load_shares(count, rows * top, bound, skew, False)
    places = jnp.arange(count)

    def named(lengths, offset_by):
        used = int((lengths > 0).sum())
        fixed = max(1, used // 4)
        moved = fixed + (places - fixed + offset_by * (used - fixed)) % max(1, count - fixed)
        return jnp.zeros((count,), jnp.int32).at[ranking[jnp.where(places < fixed, places, moved)]].set(jnp.asarray(lengths, jnp.int32))

    lengths = jnp.where(number % 4 == 0, named(packed, number // 4), named(usual, number - number // 4 - 1))
    mixed = jax.random.permutation(jax.random.fold_in(own, 3), count)
    donor, taker = mixed[0:count // 2 * 2:2], mixed[1:count // 2 * 2:2]
    room = jnp.minimum(lengths[donor] - 1, bound - lengths[taker]) // 2
    room = jnp.where((donor == ranking[0]) | (taker == ranking[0]) | (lengths[taker] == 0), 0, jnp.maximum(room, 0))
    moved = jax.random.randint(jax.random.fold_in(own, 4), (count // 2,), 0, 1 << 20) % (room + 1)
    lengths = lengths.at[donor].add(-moved).at[taker].add(moved)
    items = jnp.searchsorted(jnp.cumsum(lengths), jnp.arange(rows * top), side="right").astype(jnp.int32)
    grid = items.reshape(top, rows).T
    grid = grid[jax.random.permutation(jax.random.fold_in(own, 1), rows)]
    offset_by = jax.random.randint(jax.random.fold_in(own, 2), (rows, 1), 0, top)
    return jnp.take_along_axis(grid, (jnp.arange(top)[None, :] + offset_by) % top, axis=1)


def load_shares(amount, total, limit, skew, full):
    portions = [(1 << 20) // math.isqrt(rank ** skew) + 1 for rank in range(1, amount + 1)]
    largest = limit if full else min(limit, max(-(-total // amount), total * portions[0] // sum(portions)))
    least = 1 if total - largest >= amount - 1 else 0
    given, surplus = [largest] + [least] * (amount - 1), total - largest - least * (amount - 1)
    while surplus > 0:
        candidates = [i for i in range(1, amount) if given[i] < largest] or [i for i in range(1, amount) if given[i] < limit]
        pool, budget = sum([portions[i] for i in candidates]), surplus
        for i in candidates:
            more = min(limit - given[i], max(1, budget * portions[i] // pool), surplus)
            given[i] = given[i] + more
            surplus = surplus - more
    return np.array(given)


def noise(stream_key, extent, spread, most, split=(), held_as=jnp.bfloat16):
    drawn = spread * jax.random.normal(stream_key, extent, jnp.float32)
    if split:
        drawn = drawn * block_scale(stream_key, extent, split, -0.22, 0.18)
    return jnp.clip(drawn, -most, most).astype(held_as)


def setup_inputs(seed: int = 0) -> dict:
    streams_of = jax.random.split(jax.random.key(seed), 4)
    embeddings = noise(streams_of[0], (ROWS, D), 1.0, 6.0, ((0, 32),))
    list_ids_keys = jax.random.split(jax.random.fold_in(streams_of[1], 1), ROWS // R_DEV)
    list_ids_turns = jax.random.permutation(jax.random.fold_in(streams_of[1], 3), ROWS // R_DEV)
    list_ids = jax.vmap(lambda own, number: routed_block(jax.random.fold_in(streams_of[1], 2), own, number, R_DEV, LISTS, 1, CAP, 2))(list_ids_keys, list_ids_turns).reshape((ROWS, 1))
    centroids = noise(streams_of[2], (LISTS, FINE, D), 1.0, 6.0, ((0, 4),))
    return dict(embeddings=embeddings, list_ids=list_ids, centroids=centroids)


SHARP = 0.1
PRIOR = 1.0


def list_stats(block, live, cents):
    raw = jnp.dot(block, cents.T, preferred_element_type=jnp.float32)
    cent_sq = jnp.sum(jnp.square(cents.astype(jnp.float32)), axis=1)
    scores = SHARP * raw - 0.5 * SHARP * cent_sq[None, :]
    resp = jax.nn.softmax(scores, axis=-1) * live[:, None]
    resp = resp.astype(jnp.bfloat16)
    sums = jnp.dot(resp.T, block, preferred_element_type=jnp.float32)
    mass = jnp.sum(resp.astype(jnp.float32), axis=0)
    return sums, mass


def reference(embeddings, list_ids, centroids):
    ids = list_ids[:, 0]
    width = N_LIST * N_SHARD * CAP
    order = jnp.argsort(ids, stable=True)
    ordered = embeddings[order]
    padded = jnp.concatenate([ordered, jnp.zeros((width, D), jnp.bfloat16)], axis=0)
    counts = jnp.sum((ids[:, None] == jnp.arange(LISTS, dtype=jnp.int32)[None, :]).astype(jnp.int32), axis=0)
    starts = (jnp.cumsum(counts) - counts).astype(jnp.int32)

    def one_list(index):
        block = lax.dynamic_slice_in_dim(padded, starts[index], width, 0)
        live = (jnp.arange(width, dtype=jnp.int32) < counts[index]).astype(jnp.float32)
        cents = centroids[index]
        sums, mass = list_stats(block, live, cents)
        return (sums + PRIOR * cents.astype(jnp.float32)) / (mass[:, None] + PRIOR)

    return lax.map(one_list, jnp.arange(LISTS, dtype=jnp.int32))
```

```python
import functools

import jax
import jax.numpy as jnp
from jax import lax
from jax.experimental import pallas as pl
from jax.experimental.pallas import tpu as pltpu
from jax.sharding import PartitionSpec as P

SHARP = 0.1
PRIOR = 1.0
MESH = pl.DeviceIdType.MESH
F32 = jnp.float32
BF16 = jnp.bfloat16
CORES = 2


def iota(shape, axis):
    return lax.broadcasted_iota(jnp.int32, shape, axis)


def dot(a, b):
    return jnp.dot(a, b, preferred_element_type=F32)


def kernel(
    n_list, n_shard, full,
    ids_ref, emb_ref, cent_ref, out_ref,
    slot_s, send, recv, cbuf, csq, acc,
    part, mpart, other, mother, merged, mmerged, fin, mfin,
    cent_sem, p1_send, p1_recv, part_send, part_recv, mp_sem,
    fin_send, fin_recv, mf_send, mf_recv,
):
    local_lists, fine, width = cent_ref.shape
    quad = local_lists * CORES
    planes = n_list // CORES
    lists = planes * quad
    groups = n_shard // quad
    halves = n_shard // CORES
    per_group = quad // CORES
    share = fine // n_shard
    rows = emb_ref.shape[0]
    cap = rows // 8
    li, sh = lax.axis_index("list"), lax.axis_index("shard")
    y, core = li // CORES, li % CORES
    group, member = sh // quad, sh % quad
    home, hidx = member // local_lists, member % local_lists
    partner = {"list": y * CORES + (1 - core), "shard": sh}

    barrier = pltpu.get_barrier_semaphore()
    in_plane = CORES * n_shard

    def greet_plane(i, c):
        at = (core * n_shard + sh + i) % in_plane
        pl.semaphore_signal(
            barrier, inc=1, device_id={"list": y * CORES + at // n_shard, "shard": at % n_shard}, device_id_type=MESH
        )
        return c

    def greet_far(i, c):
        to_y = (y + 1 + i // quad) % planes
        pl.semaphore_signal(
            barrier, inc=1, device_id={"list": to_y * CORES + core, "shard": group * quad + i % quad}, device_id_type=MESH
        )
        return c

    lax.fori_loop(1, in_plane, greet_plane, 0)
    lax.fori_loop(0, (planes - 1) * quad, greet_far, 0)

    ids = ids_ref[...]
    blocks, lane = ids.shape
    hot = [jnp.where(ids == l, 1.0, 0.0).astype(F32) for l in range(lists)]
    hots = jnp.concatenate(hot, axis=0).astype(BF16)
    many = lists * blocks
    before = jnp.where(iota((lane, lane), 0) < iota((lane, lane), 1), 1.0, 0.0).astype(BF16)
    rank = dot(hots, before)
    totals = dot(hots, jnp.ones((lane, lane), BF16)).astype(BF16)
    up, down = iota((many, many), 0), iota((many, many), 1)
    earlier = jnp.where((up // blocks == down // blocks) & (down < up), 1.0, 0.0).astype(BF16)
    rank = rank + dot(earlier, totals)
    slot = jnp.zeros((blocks, lane), F32)
    for l in range(lists):
        slot = slot + hot[l] * (rank[l * blocks:(l + 1) * blocks] + float(l * cap))
    slot_s[...] = slot

    pl.semaphore_wait(barrier, in_plane - 1 + (planes - 1) * quad)

    cent_far = pltpu.make_async_remote_copy(
        src_ref=cent_ref.at[hidx], dst_ref=cbuf, send_sem=cent_sem.at[0], recv_sem=cent_sem.at[1],
        device_id=partner, device_id_type=MESH,
    )
    cent_near = pltpu.make_async_copy(cent_ref.at[hidx], cbuf, cent_sem.at[2])

    @pl.when(core == home)
    def _():
        cent_far.start()
        cent_near.start()

    def gather_rows(l, dst):
        base = (l * cap).astype(F32)
        place = iota((cap, lane), 0).astype(F32) + base
        pick = jnp.concatenate(
            [jnp.where(place == slot_s[b:b + 1, :], 1.0, 0.0).astype(BF16) for b in range(blocks)], axis=1
        )
        dst[:, :width] = dot(pick, emb_ref[...]).astype(BF16)
        if not full:
            dst[:, width:] = dot(pick, jnp.ones((rows, 128), BF16)).astype(BF16)

    def order(i):
        return (5 * i) % lists

    def row_copy(j):
        to_y, to_member = (y + j // quad) % planes, (member + j % quad) % quad
        return pltpu.make_async_remote_copy(
            src_ref=send.at[j], dst_ref=recv.at[j], send_sem=p1_send.at[j], recv_sem=p1_recv.at[j],
            device_id={"list": to_y * CORES + core, "shard": group * quad + to_member}, device_id_type=MESH,
        )

    def route(i, c):
        j = order(i)
        to_y, to_member = (y + j // quad) % planes, (member + j % quad) % quad
        gather_rows(to_y * quad + to_member, send.at[j])
        row_copy(j).start()
        return c

    lax.fori_loop(1, lists, route, 0)
    gather_rows(y * quad + member, recv.at[0])

    @pl.when(core == home)
    def _():
        cent_near.wait()

    @pl.when(core != home)
    def _():
        cent_far.wait_recv()

    def square(i, c):
        at = pl.ds(pl.multiple_of(i * 128, 128), 128)
        some = cbuf[at, :].astype(F32)
        csq[at, :] = jnp.broadcast_to((0.5 * SHARP) * jnp.sum(some * some, axis=1, keepdims=True), (128, cap))
        return c

    lax.fori_loop(0, fine // 128, square, 0)
    acc[...] = jnp.zeros_like(acc)

    def add_block(j):
        x = recv[j, :, :width]
        flags = jnp.ones((cap, 128), BF16) if full else recv[j, :, width:]
        raw = lax.dot_general(cbuf[...], x, (((1,), (1,)), ((), ())), preferred_element_type=F32)
        scores = SHARP * raw - csq[...]
        grown = jnp.exp(scores - jnp.max(scores, axis=0, keepdims=True))
        resp = (grown * (1.0 / jnp.sum(grown, axis=0, keepdims=True))).astype(BF16)
        acc[:, :width] += dot(resp, x)
        acc[:, width:] += dot(resp, flags)

    add_block(0)

    def take(i, c):
        j = order(i)
        row_copy(j).wait_recv()
        add_block(j)
        return c

    lax.fori_loop(1, lists, take, 0)

    eye = iota((share, 128), 0) == iota((share, 128), 1)

    def pair(t):
        return ((group + 1 + t // per_group) % groups) * per_group + (t + sh // CORES) % per_group

    def fine_rows(shard):
        return pl.ds(pl.multiple_of(shard * share, share), share)

    def mass_row(at):
        tile = acc[at, width:]
        return jnp.broadcast_to(jnp.sum(jnp.where(eye, tile, 0.0), axis=0, keepdims=True), (8, 128))

    def part_copy(t):
        return pltpu.make_async_remote_copy(
            src_ref=part.at[t], dst_ref=other.at[t], send_sem=part_send.at[t], recv_sem=part_recv.at[t],
            device_id=partner, device_id_type=MESH,
        )

    mass_copy = pltpu.make_async_remote_copy(
        src_ref=mpart, dst_ref=mother, send_sem=mp_sem.at[0], recv_sem=mp_sem.at[1],
        device_id=partner, device_id_type=MESH,
    )

    def give(t, c):
        at = fine_rows(CORES * pair(t) + (1 - core))
        part[t] = acc[at, :width].astype(BF16)
        part_copy(t).start()
        mpart[t] = mass_row(at)
        return c

    lax.fori_loop(0, halves, give, 0)
    mass_copy.start()

    def fin_copies(t):
        to = {"list": y * CORES + home, "shard": CORES * pair(t) + core}
        at = hidx * groups + group
        return [
            pltpu.make_async_remote_copy(
                src_ref=src.at[t], dst_ref=dst.at[at], send_sem=ss.at[t], recv_sem=rs.at[at],
                device_id=to, device_id_type=MESH,
            )
            for src, dst, ss, rs in ((merged, fin, fin_send, fin_recv), (mmerged, mfin, mf_send, mf_recv))
        ]

    def own_copies(t):
        at = hidx * groups + group
        return [
            pltpu.make_async_copy(merged.at[t], fin.at[at], fin_recv.at[at]),
            pltpu.make_async_copy(mmerged.at[t], mfin.at[at], mf_recv.at[at]),
        ]

    def is_own(t):
        return (home == core) & (CORES * pair(t) + core == sh)

    mass_copy.wait_recv()

    def forward(t, c):
        at = fine_rows(CORES * pair(t) + core)
        part_copy(t).wait_recv()
        merged[t] = (acc[at, :width] + other[t].astype(F32)).astype(BF16)
        mmerged[t] = mass_row(at) + mother[t]

        @pl.when(is_own(t))
        def _():
            for copy in own_copies(t):
                copy.start()

        @pl.when(jnp.logical_not(is_own(t)))
        def _():
            for copy in fin_copies(t):
                copy.start()

        return c

    lax.fori_loop(0, halves, forward, 0)

    @pl.when(core == home)
    def _():
        cent_far.wait_send()

    def sent_rows(i, c):
        row_copy(order(i)).wait_send()
        return c

    lax.fori_loop(1, lists, sent_rows, 0)

    def sent_parts(t, c):
        part_copy(t).wait_send()
        return c

    lax.fori_loop(0, halves, sent_parts, 0)
    mass_copy.wait_send()

    def arrived(i):
        return [
            pltpu.make_async_copy(fin.at[i], fin.at[i], fin_recv.at[i]),
            pltpu.make_async_copy(mfin.at[i], mfin.at[i], mf_recv.at[i]),
        ]

    for h in range(local_lists):
        sums = cent_ref[h, fine_rows(sh), :].astype(F32) * PRIOR
        mass = jnp.zeros((1, 128), F32)
        for k in range(groups):
            i = h * groups + k
            for copy in arrived(i):
                copy.wait()
            sums = sums + fin[i].astype(F32)
            mass = mass + mfin[i, 0:1, :]
        column = jnp.sum(jnp.where(eye, mass, 0.0), axis=1, keepdims=True)
        out_ref[h] = sums / (column + PRIOR)

    def sent_fin(t, c):
        @pl.when(jnp.logical_not(is_own(t)))
        def _():
            for copy in fin_copies(t):
                copy.wait_send()

        return c

    lax.fori_loop(0, halves, sent_fin, 0)


def solution(mesh):
    n_list, n_shard = mesh.shape["list"], mesh.shape["shard"]

    def per_device(embeddings, list_ids, centroids):
        rows, width = embeddings.shape
        local_lists, fine, _ = centroids.shape
        cap = rows // 8
        lists = local_lists * n_list
        full = lists * cap == rows
        sent = width if full else width + 128
        share = fine // n_shard
        halves = n_shard // CORES
        arrivals = local_lists * (n_shard // (local_lists * CORES))
        dma = pltpu.SemaphoreType.DMA
        vmem = pl.BlockSpec(memory_space=pltpu.VMEM)
        flops = 2 * rows * lists * cap * width + 4 * lists * cap * fine * width
        return pl.pallas_call(
            functools.partial(kernel, n_list, n_shard, full),
            out_shape=jax.ShapeDtypeStruct((local_lists, share, width), F32),
            in_specs=[vmem, vmem, vmem],
            out_specs=vmem,
            scratch_shapes=[
                pltpu.VMEM((rows // cap, cap), F32),
                pltpu.VMEM((lists, cap, sent), BF16),
                pltpu.VMEM((lists, cap, sent), BF16),
                pltpu.VMEM((fine, width), BF16),
                pltpu.VMEM((fine, cap), F32),
                pltpu.VMEM((fine, width + 128), F32),
                pltpu.VMEM((halves, share, width), BF16),
                pltpu.VMEM((halves, 8, 128), F32),
                pltpu.VMEM((halves, share, width), BF16),
                pltpu.VMEM((halves, 8, 128), F32),
                pltpu.VMEM((halves, share, width), BF16),
                pltpu.VMEM((halves, 8, 128), F32),
                pltpu.VMEM((arrivals, share, width), BF16),
                pltpu.VMEM((arrivals, 8, 128), F32),
                dma((3,)),
                dma((lists,)),
                dma((lists,)),
                dma((halves,)),
                dma((halves,)),
                dma((2,)),
                dma((halves,)),
                dma((arrivals,)),
                dma((halves,)),
                dma((arrivals,)),
            ],
            compiler_params=pltpu.CompilerParams(
                collective_id=0, has_side_effects=True, vmem_limit_bytes=52 * 2**20
            ),
            cost_estimate=pl.CostEstimate(
                flops=flops, bytes_accessed=4 * rows * width, transcendentals=lists * cap * fine
            ),
        )(list_ids.reshape(rows // cap, cap), embeddings, centroids)

    placed = (P(("list", "shard"), None), P(("list", "shard"), None), P("list", None, None))
    return jax.shard_map(
        per_device, mesh=mesh, in_specs=placed, out_specs=P("list", "shard", None), check_vma=False
    )
```

```python
import functools

import jax
import jax.numpy as jnp
from jax import lax
from jax.experimental import pallas as pl
from jax.experimental.pallas import tpu as pltpu
from jax.sharding import PartitionSpec as P

SHARP = 0.1
PRIOR = 1.0
MESH = pl.DeviceIdType.MESH
F32 = jnp.float32
BF16 = jnp.bfloat16
CORES = 2
AHEAD = 3


def iota(shape, axis):
    return lax.broadcasted_iota(jnp.int32, shape, axis)


def dot(a, b):
    return jnp.dot(a, b, preferred_element_type=F32)


def kernel(
    n_list, n_shard, full,
    ids_ref, emb_ref, cent_ref, out_ref,
    emb_s, own_s, slot_s, send, recv, cbuf, csq, acc,
    part, mpart, other, mother, merged, mmerged, fin, mfin,
    in_sem, cent_sem, p1_send, p1_recv, part_send, part_recv, mp_sem,
    fin_send, fin_recv, mf_send, mf_recv,
):
    local_lists, fine, width = cent_ref.shape
    quad = local_lists * CORES
    planes = n_list // CORES
    lists = planes * quad
    groups = n_shard // quad
    halves = n_shard // CORES
    per_group = quad // CORES
    share = fine // n_shard
    rows = emb_ref.shape[0]
    cap = rows // 8
    li, sh = lax.axis_index("list"), lax.axis_index("shard")
    y, core = li // CORES, li % CORES
    group, member = sh // quad, sh % quad
    home, hidx = member // local_lists, member % local_lists
    partner = {"list": y * CORES + (1 - core), "shard": sh}

    emb_in = pltpu.make_async_copy(emb_ref, emb_s, in_sem.at[0])
    own_in = pltpu.make_async_copy(
        cent_ref.at[:, pl.ds(pl.multiple_of(sh * share, share), share), :], own_s, in_sem.at[1]
    )
    emb_in.start()
    own_in.start()

    barrier = pltpu.get_barrier_semaphore()
    in_plane = CORES * n_shard

    def greet_plane(i, c):
        at = (core * n_shard + sh + i) % in_plane
        pl.semaphore_signal(
            barrier, inc=1, device_id={"list": y * CORES + at // n_shard, "shard": at % n_shard}, device_id_type=MESH
        )
        return c

    def greet_far(i, c):
        to_y = (y + 1 + i // quad) % planes
        pl.semaphore_signal(
            barrier, inc=1, device_id={"list": to_y * CORES + core, "shard": group * quad + i % quad}, device_id_type=MESH
        )
        return c

    lax.fori_loop(1, in_plane, greet_plane, 0)
    lax.fori_loop(0, (planes - 1) * quad, greet_far, 0)

    blocks, lane = rows // cap, cap
    ids = jnp.concatenate([ids_ref[:, b * lane:(b + 1) * lane] for b in range(blocks)], axis=0)
    hot = [jnp.where(ids == l, 1.0, 0.0).astype(F32) for l in range(lists)]
    hots = jnp.concatenate(hot, axis=0).astype(BF16)
    many = lists * blocks
    before = jnp.where(iota((lane, lane), 0) < iota((lane, lane), 1), 1.0, 0.0).astype(BF16)
    rank = dot(hots, before)
    totals = dot(hots, jnp.ones((lane, lane), BF16)).astype(BF16)
    up, down = iota((many, many), 0), iota((many, many), 1)
    earlier = jnp.where((up // blocks == down // blocks) & (down < up), 1.0, 0.0).astype(BF16)
    rank = rank + dot(earlier, totals)
    slot = jnp.zeros((blocks, lane), F32)
    for l in range(lists):
        slot = slot + hot[l] * (rank[l * blocks:(l + 1) * blocks] + float(l * cap))
    slot_s[...] = slot

    emb_in.wait()
    pl.semaphore_wait(barrier, in_plane - 1 + (planes - 1) * quad)

    cent_far = pltpu.make_async_remote_copy(
        src_ref=cent_ref.at[hidx], dst_ref=cbuf, send_sem=cent_sem.at[0], recv_sem=cent_sem.at[1],
        device_id=partner, device_id_type=MESH,
    )
    cent_near = pltpu.make_async_copy(cent_ref.at[hidx], cbuf, cent_sem.at[2])

    @pl.when(core == home)
    def _():
        cent_far.start()
        cent_near.start()

    def gather_rows(l, dst):
        base = (l * cap).astype(F32)
        place = iota((cap, lane), 0).astype(F32) + base
        pick = jnp.concatenate(
            [jnp.where(place == slot_s[b:b + 1, :], 1.0, 0.0).astype(BF16) for b in range(blocks)], axis=1
        )
        dst[:, :width] = dot(pick, emb_s[...]).astype(BF16)
        if not full:
            dst[:, width:] = dot(pick, jnp.ones((rows, 128), BF16)).astype(BF16)

    def order(i):
        return lists // 2 + i // 2 - (i % 2) * (2 * (i // 2) + 1)

    def target(j):
        flip = j % quad
        to_member = ((member // 2 + flip // 2) % (quad // 2)) * 2 + (member + flip) % 2
        return (y + j // quad) % planes, to_member

    def row_copy(j):
        to_y, to_member = target(j)
        return pltpu.make_async_remote_copy(
            src_ref=send.at[j], dst_ref=recv.at[j], send_sem=p1_send.at[j], recv_sem=p1_recv.at[j],
            device_id={"list": to_y * CORES + core, "shard": group * quad + to_member}, device_id_type=MESH,
        )

    def prepare(i):
        to_y, to_member = target(order(i))
        gather_rows(to_y * quad + to_member, send.at[order(i)])

    def route(i, c):
        prepare(i)
        row_copy(order(i)).start()
        return c

    def hold(i, c):
        prepare(i)
        return c

    lax.fori_loop(0, AHEAD, route, 0)
    lax.fori_loop(AHEAD, lists - 1, hold, 0)
    gather_rows(y * quad + member, recv.at[0])

    @pl.when(core == home)
    def _():
        cent_near.wait()

    @pl.when(core != home)
    def _():
        cent_far.wait_recv()

    def square(i, c):
        at = pl.ds(pl.multiple_of(i * 128, 128), 128)
        some = cbuf[at, :].astype(F32)
        csq[at, :] = jnp.broadcast_to((0.5 * SHARP) * jnp.sum(some * some, axis=1, keepdims=True), (128, cap))
        return c

    lax.fori_loop(0, fine // 128, square, 0)
    acc[...] = jnp.zeros_like(acc)

    def add_block(j):
        x = recv[j, :, :width]
        flags = jnp.ones((cap, 128), BF16) if full else recv[j, :, width:]
        raw = lax.dot_general(cbuf[...], x, (((1,), (1,)), ((), ())), preferred_element_type=F32)
        scores = SHARP * raw - csq[...]
        grown = jnp.exp(scores - jnp.max(scores, axis=0, keepdims=True))
        resp = (grown * (1.0 / jnp.sum(grown, axis=0, keepdims=True))).astype(BF16)
        acc[:, :width] += dot(resp, x)
        acc[:, width:] += dot(resp, flags)

    add_block(0)

    def take(i, c):
        j = order(i)
        row_copy(j).wait_send()

        @pl.when(i + AHEAD < lists - 1)
        def _():
            row_copy(order(i + AHEAD)).start()

        row_copy(j).wait_recv()
        add_block(j)
        return c

    lax.fori_loop(0, lists - 1, take, 0)

    eye = iota((share, 128), 0) == iota((share, 128), 1)

    def pair(t):
        return ((group + 1 + t // per_group) % groups) * per_group + (t + sh // CORES) % per_group

    def fine_rows(shard):
        return pl.ds(pl.multiple_of(shard * share, share), share)

    def mass_row(at):
        tile = acc[at, width:]
        return jnp.broadcast_to(jnp.sum(jnp.where(eye, tile, 0.0), axis=0, keepdims=True), (8, 128))

    def part_copy(t):
        return pltpu.make_async_remote_copy(
            src_ref=part.at[t], dst_ref=other.at[t], send_sem=part_send.at[t], recv_sem=part_recv.at[t],
            device_id=partner, device_id_type=MESH,
        )

    mass_copy = pltpu.make_async_remote_copy(
        src_ref=mpart, dst_ref=mother, send_sem=mp_sem.at[0], recv_sem=mp_sem.at[1],
        device_id=partner, device_id_type=MESH,
    )

    def give(t, c):
        at = fine_rows(CORES * pair(t) + (1 - core))
        part[t] = acc[at, :width].astype(BF16)
        part_copy(t).start()
        mpart[t] = mass_row(at)
        return c

    lax.fori_loop(0, halves, give, 0)
    mass_copy.start()

    def fin_copies(t):
        to = {"list": y * CORES + home, "shard": CORES * pair(t) + core}
        at = hidx * groups + group
        return [
            pltpu.make_async_remote_copy(
                src_ref=src.at[t], dst_ref=dst.at[at], send_sem=ss.at[t], recv_sem=rs.at[at],
                device_id=to, device_id_type=MESH,
            )
            for src, dst, ss, rs in ((merged, fin, fin_send, fin_recv), (mmerged, mfin, mf_send, mf_recv))
        ]

    def own_copies(t):
        at = hidx * groups + group
        return [
            pltpu.make_async_copy(merged.at[t], fin.at[at], fin_recv.at[at]),
            pltpu.make_async_copy(mmerged.at[t], mfin.at[at], mf_recv.at[at]),
        ]

    def is_own(t):
        return (home == core) & (CORES * pair(t) + core == sh)

    mass_copy.wait_recv()

    def forward(t, c):
        at = fine_rows(CORES * pair(t) + core)
        part_copy(t).wait_recv()
        merged[t] = (acc[at, :width] + other[t].astype(F32)).astype(BF16)
        mmerged[t] = mass_row(at) + mother[t]

        @pl.when(is_own(t))
        def _():
            for copy in own_copies(t):
                copy.start()

        @pl.when(jnp.logical_not(is_own(t)))
        def _():
            for copy in fin_copies(t):
                copy.start()

        return c

    lax.fori_loop(0, halves, forward, 0)

    @pl.when(core == home)
    def _():
        cent_far.wait_send()

    def sent_parts(t, c):
        part_copy(t).wait_send()
        return c

    lax.fori_loop(0, halves, sent_parts, 0)
    mass_copy.wait_send()

    def arrived(i):
        return [
            pltpu.make_async_copy(fin.at[i], fin.at[i], fin_recv.at[i]),
            pltpu.make_async_copy(mfin.at[i], mfin.at[i], mf_recv.at[i]),
        ]

    own_in.wait()
    for h in range(local_lists):
        sums = own_s[h].astype(F32) * PRIOR
        mass = jnp.zeros((1, 128), F32)
        for k in range(groups):
            i = h * groups + k
            for copy in arrived(i):
                copy.wait()
            sums = sums + fin[i].astype(F32)
            mass = mass + mfin[i, 0:1, :]
        column = jnp.sum(jnp.where(eye, mass, 0.0), axis=1, keepdims=True)
        out_ref[h] = sums / (column + PRIOR)

    def sent_fin(t, c):
        @pl.when(jnp.logical_not(is_own(t)))
        def _():
            for copy in fin_copies(t):
                copy.wait_send()

        return c

    lax.fori_loop(0, halves, sent_fin, 0)


def solution(mesh):
    n_list, n_shard = mesh.shape["list"], mesh.shape["shard"]

    def per_device(embeddings, list_ids, centroids):
        rows, width = embeddings.shape
        local_lists, fine, _ = centroids.shape
        cap = rows // 8
        lists = local_lists * n_list
        full = lists * cap == rows
        sent = width if full else width + 128
        share = fine // n_shard
        halves = n_shard // CORES
        arrivals = local_lists * (n_shard // (local_lists * CORES))
        dma = pltpu.SemaphoreType.DMA
        vmem = pl.BlockSpec(memory_space=pltpu.VMEM)
        flops = 2 * rows * lists * cap * width + 4 * lists * cap * fine * width
        return pl.pallas_call(
            functools.partial(kernel, n_list, n_shard, full),
            out_shape=jax.ShapeDtypeStruct((local_lists, share, width), F32),
            in_specs=[vmem, pl.BlockSpec(memory_space=pl.ANY), pl.BlockSpec(memory_space=pl.ANY)],
            out_specs=vmem,
            scratch_shapes=[
                pltpu.VMEM((rows, width), BF16),
                pltpu.VMEM((local_lists, share, width), BF16),
                pltpu.VMEM((rows // cap, cap), F32),
                pltpu.VMEM((lists, cap, sent), BF16),
                pltpu.VMEM((lists, cap, sent), BF16),
                pltpu.VMEM((fine, width), BF16),
                pltpu.VMEM((fine, cap), F32),
                pltpu.VMEM((fine, width + 128), F32),
                pltpu.VMEM((halves, share, width), BF16),
                pltpu.VMEM((halves, 8, 128), F32),
                pltpu.VMEM((halves, share, width), BF16),
                pltpu.VMEM((halves, 8, 128), F32),
                pltpu.VMEM((halves, share, width), BF16),
                pltpu.VMEM((halves, 8, 128), F32),
                pltpu.VMEM((arrivals, share, width), BF16),
                pltpu.VMEM((arrivals, 8, 128), F32),
                dma((2,)),
                dma((3,)),
                dma((lists,)),
                dma((lists,)),
                dma((halves,)),
                dma((halves,)),
                dma((2,)),
                dma((halves,)),
                dma((arrivals,)),
                dma((halves,)),
                dma((arrivals,)),
            ],
            compiler_params=pltpu.CompilerParams(
                collective_id=0, has_side_effects=True, vmem_limit_bytes=52 * 2**20
            ),
            cost_estimate=pl.CostEstimate(
                flops=flops, bytes_accessed=4 * rows * width, transcendentals=lists * cap * fine
            ),
        )(list_ids.T, embeddings, centroids)

    placed = (P(("list", "shard"), None), P(("list", "shard"), None), P("list", None, None))
    return jax.shard_map(
        per_device, mesh=mesh, in_specs=placed, out_specs=P("list", "shard", None), check_vma=False
    )
```

```python
import functools

import jax
import jax.numpy as jnp
from jax import lax
from jax.experimental import pallas as pl
from jax.experimental.pallas import tpu as pltpu
from jax.sharding import PartitionSpec as P

SHARP = 0.1
PRIOR = 1.0
MESH = pl.DeviceIdType.MESH
F32 = jnp.float32
BF16 = jnp.bfloat16
CORES = 2
AHEAD = 4


def iota(shape, axis):
    return lax.broadcasted_iota(jnp.int32, shape, axis)


def dot(a, b):
    return jnp.dot(a, b, preferred_element_type=F32)


def kernel(
    n_list, n_shard, full,
    ids_ref, emb_ref, cent_ref, out_ref,
    emb_s, own_s, resp_s, slot_s, send, recv, cbuf, csq, acc,
    part, mpart, other, mother, merged, mmerged, fin, mfin,
    in_sem, cent_sem, p1_send, p1_recv, part_send, part_recv, mp_sem,
    fin_send, fin_recv, mf_send, mf_recv,
):
    local_lists, _, _, share, width = cent_ref.shape
    fine = n_shard * share
    quad = local_lists * CORES
    planes = n_list // CORES
    lists = planes * quad
    groups = n_shard // quad
    halves = n_shard // CORES
    per_group = quad // CORES
    half = halves * share
    rows = emb_ref.shape[0]
    cap = rows // 8
    li, sh = lax.axis_index("list"), lax.axis_index("shard")
    y, core = li // CORES, li % CORES
    group, member = sh // quad, sh % quad
    home, hidx = member // local_lists, member % local_lists
    partner = {"list": y * CORES + (1 - core), "shard": sh}

    emb_in = pltpu.make_async_copy(emb_ref, emb_s, in_sem.at[0])
    own_in = pltpu.make_async_copy(cent_ref.at[:, sh // CORES, sh % CORES], own_s, in_sem.at[1])
    emb_in.start()
    own_in.start()

    barrier = pltpu.get_barrier_semaphore()
    in_plane = CORES * n_shard

    def greet_plane(i, c):
        at = (core * n_shard + sh + i) % in_plane
        pl.semaphore_signal(
            barrier, inc=1, device_id={"list": y * CORES + at // n_shard, "shard": at % n_shard}, device_id_type=MESH
        )
        return c

    def greet_far(i, c):
        to_y = (y + 1 + i // quad) % planes
        pl.semaphore_signal(
            barrier, inc=1, device_id={"list": to_y * CORES + core, "shard": group * quad + i % quad}, device_id_type=MESH
        )
        return c

    lax.fori_loop(1, in_plane, greet_plane, 0)
    lax.fori_loop(0, (planes - 1) * quad, greet_far, 0)

    blocks, lane = rows // cap, cap
    ids = jnp.concatenate([ids_ref[:, b * lane:(b + 1) * lane] for b in range(blocks)], axis=0)
    hot = [jnp.where(ids == l, 1.0, 0.0).astype(F32) for l in range(lists)]
    hots = jnp.concatenate(hot, axis=0).astype(BF16)
    many = lists * blocks
    before = jnp.where(iota((lane, lane), 0) < iota((lane, lane), 1), 1.0, 0.0).astype(BF16)
    rank = dot(hots, before)
    totals = dot(hots, jnp.ones((lane, lane), BF16)).astype(BF16)
    up, down = iota((many, many), 0), iota((many, many), 1)
    earlier = jnp.where((up // blocks == down // blocks) & (down < up), 1.0, 0.0).astype(BF16)
    rank = rank + dot(earlier, totals)
    slot = jnp.zeros((blocks, lane), F32)
    for l in range(lists):
        slot = slot + hot[l] * (rank[l * blocks:(l + 1) * blocks] + float(l * cap))
    slot_s[...] = slot

    emb_in.wait()
    pl.semaphore_wait(barrier, in_plane - 1 + (planes - 1) * quad)

    cent_far = [
        pltpu.make_async_remote_copy(
            src_ref=cent_ref.at[hidx, :, p], dst_ref=cbuf.at[p], send_sem=cent_sem.at[0, p], recv_sem=cent_sem.at[1, p],
            device_id=partner, device_id_type=MESH,
        )
        for p in range(CORES)
    ]
    cent_near = [
        pltpu.make_async_copy(cent_ref.at[hidx, :, p], cbuf.at[p], cent_sem.at[2, p]) for p in range(CORES)
    ]

    @pl.when(core == home)
    def _():
        for copy in cent_far + cent_near:
            copy.start()

    def gather_rows(l, dst):
        base = (l * cap).astype(F32)
        place = iota((cap, lane), 0).astype(F32) + base
        pick = jnp.concatenate(
            [jnp.where(place == slot_s[b:b + 1, :], 1.0, 0.0).astype(BF16) for b in range(blocks)], axis=1
        )
        dst[:, :width] = dot(pick, emb_s[...]).astype(BF16)
        if not full:
            dst[:, width:] = dot(pick, jnp.ones((rows, 128), BF16)).astype(BF16)

    def order(i):
        return lists // 2 + i // 2 - (i % 2) * (2 * (i // 2) + 1)

    def target(j):
        flip = j % quad
        to_member = ((member // 2 + flip // 2) % (quad // 2)) * 2 + (member + flip) % 2
        return (y + j // quad) % planes, to_member

    def row_copy(j):
        to_y, to_member = target(j)
        return pltpu.make_async_remote_copy(
            src_ref=send.at[j], dst_ref=recv.at[j], send_sem=p1_send.at[j], recv_sem=p1_recv.at[j],
            device_id={"list": to_y * CORES + core, "shard": group * quad + to_member}, device_id_type=MESH,
        )

    def prepare(i):
        to_y, to_member = target(order(i))
        gather_rows(to_y * quad + to_member, send.at[order(i)])

    def route(i, c):
        prepare(i)
        row_copy(order(i)).start()
        return c

    def hold(i, c):
        prepare(i)
        return c

    lax.fori_loop(0, AHEAD, route, 0)
    lax.fori_loop(AHEAD, lists - 1, hold, 0)
    gather_rows(y * quad + member, recv.at[0])

    @pl.when(core == home)
    def _():
        for copy in cent_near:
            copy.wait()

    @pl.when(core != home)
    def _():
        for copy in cent_far:
            copy.wait_recv()

    def square(i, c):
        at = pl.ds(pl.multiple_of(i * share, share), share)
        some = cbuf[i // halves, i % halves].astype(F32)
        csq[at, :] = jnp.broadcast_to((0.5 * SHARP) * jnp.sum(some * some, axis=1, keepdims=True), (share, cap))
        return c

    lax.fori_loop(0, n_shard, square, 0)
    acc[...] = jnp.zeros_like(acc)

    def responses(j):
        cents = cbuf[...].reshape(fine, width)
        raw = lax.dot_general(
            cents, recv[j, :, :width], (((1,), (1,)), ((), ())), preferred_element_type=F32
        )
        scores = SHARP * raw - csq[...]
        grown = jnp.exp(scores - jnp.max(scores, axis=0, keepdims=True))
        return (grown * (1.0 / jnp.sum(grown, axis=0, keepdims=True))).astype(BF16)

    def add(j, at, resp):
        acc[at, :width] += dot(resp, recv[j, :, :width])
        acc[at, width:] += dot(resp, jnp.ones((cap, 128), BF16) if full else recv[j, :, width:])

    add(0, slice(None), responses(0))

    def await_rows(i):
        row_copy(order(i)).wait_send()

        @pl.when(i + AHEAD < lists - 1)
        def _():
            row_copy(order(i + AHEAD)).start()

        row_copy(order(i)).wait_recv()

    def take(i, c):
        await_rows(i)
        add(order(i), slice(None), responses(order(i)))
        return c

    lax.fori_loop(0, lists - 2, take, 0)

    final = lists - 2
    await_rows(final)
    resp_s[...] = responses(order(final))

    def add_last(p):
        at = pl.ds(pl.multiple_of(p * half, half), half)
        add(order(final), at, resp_s[at, :])

    add_last(1 - core)

    eye = iota((share, 128), 0) == iota((share, 128), 1)

    def pair(t):
        return ((group + 1 + t // per_group) % groups) * per_group + (t + sh // CORES) % per_group

    def fine_rows(p, t):
        return pl.ds(pl.multiple_of(p * half + pair(t) * share, share), share)

    def mass_row(at):
        tile = acc[at, width:]
        return jnp.broadcast_to(jnp.sum(jnp.where(eye, tile, 0.0), axis=0, keepdims=True), (8, 128))

    def part_copy(t):
        return pltpu.make_async_remote_copy(
            src_ref=part.at[t], dst_ref=other.at[t], send_sem=part_send.at[t], recv_sem=part_recv.at[t],
            device_id=partner, device_id_type=MESH,
        )

    mass_copy = pltpu.make_async_remote_copy(
        src_ref=mpart, dst_ref=mother, send_sem=mp_sem.at[0], recv_sem=mp_sem.at[1],
        device_id=partner, device_id_type=MESH,
    )

    def give(t, c):
        at = fine_rows(1 - core, t)
        part[t] = acc[at, :width].astype(BF16)
        part_copy(t).start()
        mpart[t] = mass_row(at)
        return c

    lax.fori_loop(0, halves, give, 0)
    mass_copy.start()
    add_last(core)

    def fin_copies(t):
        to = {"list": y * CORES + home, "shard": CORES * pair(t) + core}
        at = hidx * groups + group
        return [
            pltpu.make_async_remote_copy(
                src_ref=src.at[t], dst_ref=dst.at[at], send_sem=ss.at[t], recv_sem=rs.at[at],
                device_id=to, device_id_type=MESH,
            )
            for src, dst, ss, rs in ((merged, fin, fin_send, fin_recv), (mmerged, mfin, mf_send, mf_recv))
        ]

    def own_copies(t):
        at = hidx * groups + group
        return [
            pltpu.make_async_copy(merged.at[t], fin.at[at], fin_recv.at[at]),
            pltpu.make_async_copy(mmerged.at[t], mfin.at[at], mf_recv.at[at]),
        ]

    def is_own(t):
        return (home == core) & (CORES * pair(t) + core == sh)

    mass_copy.wait_recv()

    def forward(t, c):
        at = fine_rows(core, t)
        part_copy(t).wait_recv()
        merged[t] = (acc[at, :width] + other[t].astype(F32)).astype(BF16)
        mmerged[t] = mass_row(at) + mother[t]

        @pl.when(is_own(t))
        def _():
            for copy in own_copies(t):
                copy.start()

        @pl.when(jnp.logical_not(is_own(t)))
        def _():
            for copy in fin_copies(t):
                copy.start()

        return c

    lax.fori_loop(0, halves, forward, 0)

    @pl.when(core == home)
    def _():
        for copy in cent_far:
            copy.wait_send()

    def sent_parts(t, c):
        part_copy(t).wait_send()
        return c

    lax.fori_loop(0, halves, sent_parts, 0)
    mass_copy.wait_send()

    def arrived(i):
        return [
            pltpu.make_async_copy(fin.at[i], fin.at[i], fin_recv.at[i]),
            pltpu.make_async_copy(mfin.at[i], mfin.at[i], mf_recv.at[i]),
        ]

    own_in.wait()
    for h in range(local_lists):
        sums = own_s[h].astype(F32) * PRIOR
        mass = jnp.zeros((1, 128), F32)
        for k in range(groups):
            i = h * groups + k
            for copy in arrived(i):
                copy.wait()
            sums = sums + fin[i].astype(F32)
            mass = mass + mfin[i, 0:1, :]
        column = jnp.sum(jnp.where(eye, mass, 0.0), axis=1, keepdims=True)
        out_ref[h] = sums / (column + PRIOR)

    def sent_fin(t, c):
        @pl.when(jnp.logical_not(is_own(t)))
        def _():
            for copy in fin_copies(t):
                copy.wait_send()

        return c

    lax.fori_loop(0, halves, sent_fin, 0)


def solution(mesh):
    n_list, n_shard = mesh.shape["list"], mesh.shape["shard"]

    def per_device(embeddings, list_ids, centroids):
        rows, width = embeddings.shape
        local_lists, fine, _ = centroids.shape
        cap = rows // 8
        lists = local_lists * n_list
        full = lists * cap == rows
        sent = width if full else width + 128
        share = fine // n_shard
        halves = n_shard // CORES
        arrivals = local_lists * (n_shard // (local_lists * CORES))
        dma = pltpu.SemaphoreType.DMA
        vmem = pl.BlockSpec(memory_space=pltpu.VMEM)
        flops = 2 * rows * lists * cap * width + 4 * lists * cap * fine * width
        return pl.pallas_call(
            functools.partial(kernel, n_list, n_shard, full),
            out_shape=jax.ShapeDtypeStruct((local_lists, share, width), F32),
            in_specs=[vmem, pl.BlockSpec(memory_space=pl.ANY), pl.BlockSpec(memory_space=pl.ANY)],
            out_specs=vmem,
            scratch_shapes=[
                pltpu.VMEM((rows, width), BF16),
                pltpu.VMEM((local_lists, share, width), BF16),
                pltpu.VMEM((fine, cap), BF16),
                pltpu.VMEM((rows // cap, cap), F32),
                pltpu.VMEM((lists, cap, sent), BF16),
                pltpu.VMEM((lists, cap, sent), BF16),
                pltpu.VMEM((CORES, halves, share, width), BF16),
                pltpu.VMEM((fine, cap), F32),
                pltpu.VMEM((fine, width + 128), F32),
                pltpu.VMEM((halves, share, width), BF16),
                pltpu.VMEM((halves, 8, 128), F32),
                pltpu.VMEM((halves, share, width), BF16),
                pltpu.VMEM((halves, 8, 128), F32),
                pltpu.VMEM((halves, share, width), BF16),
                pltpu.VMEM((halves, 8, 128), F32),
                pltpu.VMEM((arrivals, share, width), BF16),
                pltpu.VMEM((arrivals, 8, 128), F32),
                dma((2,)),
                dma((3, CORES)),
                dma((lists,)),
                dma((lists,)),
                dma((halves,)),
                dma((halves,)),
                dma((2,)),
                dma((halves,)),
                dma((arrivals,)),
                dma((halves,)),
                dma((arrivals,)),
            ],
            compiler_params=pltpu.CompilerParams(
                collective_id=0, has_side_effects=True, vmem_limit_bytes=52 * 2**20
            ),
            cost_estimate=pl.CostEstimate(
                flops=flops, bytes_accessed=4 * rows * width, transcendentals=lists * cap * fine
            ),
        )(list_ids.T, embeddings, centroids.reshape(local_lists, halves, CORES, share, width))

    placed = (P(("list", "shard"), None), P(("list", "shard"), None), P("list", None, None))
    return jax.shard_map(
        per_device, mesh=mesh, in_specs=placed, out_specs=P("list", "shard", None), check_vma=False
    )
```

```python
import functools

import jax
import jax.numpy as jnp
from jax import lax
from jax.experimental import pallas as pl
from jax.experimental.pallas import tpu as pltpu
from jax.sharding import PartitionSpec as P

SHARP = 0.1
PRIOR = 1.0
MESH = pl.DeviceIdType.MESH
F32 = jnp.float32
BF16 = jnp.bfloat16
CORES = 2
AHEAD = 4


def iota(shape, axis):
    return lax.broadcasted_iota(jnp.int32, shape, axis)


def dot(a, b):
    return jnp.dot(a, b, preferred_element_type=F32)


def kernel(
    n_list, n_shard, full,
    ids_ref, emb_ref, cent_ref, out_ref,
    emb_s, own_s, resp_s, slot_s, send, recv, cbuf, csq, acc,
    part, mpart, other, mother, merged, mmerged, fin, mfin,
    in_sem, cent_sem, p1_send, p1_recv, part_send, part_recv, mp_sem,
    fin_send, fin_recv, mf_send, mf_recv,
):
    local_lists, _, _, share, width = cent_ref.shape
    fine = n_shard * share
    quad = local_lists * CORES
    planes = n_list // CORES
    lists = planes * quad
    groups = n_shard // quad
    halves = n_shard // CORES
    per_group = quad // CORES
    half = halves * share
    rows = emb_ref.shape[0]
    cap = rows // 8
    li, sh = lax.axis_index("list"), lax.axis_index("shard")
    y, core = li // CORES, li % CORES
    group, member = sh // quad, sh % quad
    home, hidx = member // local_lists, member % local_lists
    partner = {"list": y * CORES + (1 - core), "shard": sh}

    emb_in = pltpu.make_async_copy(emb_ref, emb_s, in_sem.at[0])
    own_in = pltpu.make_async_copy(cent_ref.at[:, sh // CORES, sh % CORES], own_s, in_sem.at[1])
    emb_in.start()
    own_in.start()

    barrier = pltpu.get_barrier_semaphore()
    in_plane = CORES * n_shard

    def greet_plane(i, c):
        at = (core * n_shard + sh + i) % in_plane
        pl.semaphore_signal(
            barrier, inc=1, device_id={"list": y * CORES + at // n_shard, "shard": at % n_shard}, device_id_type=MESH
        )
        return c

    def greet_far(i, c):
        to_y = (y + 1 + i // quad) % planes
        pl.semaphore_signal(
            barrier, inc=1, device_id={"list": to_y * CORES + core, "shard": group * quad + i % quad}, device_id_type=MESH
        )
        return c

    lax.fori_loop(1, in_plane, greet_plane, 0)
    lax.fori_loop(0, (planes - 1) * quad, greet_far, 0)

    blocks, lane = rows // cap, cap
    ids = jnp.concatenate([ids_ref[:, b * lane:(b + 1) * lane] for b in range(blocks)], axis=0)
    hot = [jnp.where(ids == l, 1.0, 0.0).astype(F32) for l in range(lists)]
    hots = jnp.concatenate(hot, axis=0).astype(BF16)
    many = lists * blocks
    before = jnp.where(iota((lane, lane), 0) < iota((lane, lane), 1), 1.0, 0.0).astype(BF16)
    rank = dot(hots, before)
    totals = dot(hots, jnp.ones((lane, lane), BF16)).astype(BF16)
    up, down = iota((many, many), 0), iota((many, many), 1)
    earlier = jnp.where((up // blocks == down // blocks) & (down < up), 1.0, 0.0).astype(BF16)
    rank = rank + dot(earlier, totals)
    slot = jnp.zeros((blocks, lane), F32)
    for l in range(lists):
        slot = slot + hot[l] * (rank[l * blocks:(l + 1) * blocks] + float(l * cap))
    slot_s[...] = slot

    emb_in.wait()

    cent_far = [
        pltpu.make_async_remote_copy(
            src_ref=cent_ref.at[hidx, :, p], dst_ref=cbuf.at[p], send_sem=cent_sem.at[0, p], recv_sem=cent_sem.at[1, p],
            device_id=partner, device_id_type=MESH,
        )
        for p in range(CORES)
    ]
    cent_near = [
        pltpu.make_async_copy(cent_ref.at[hidx, :, p], cbuf.at[p], cent_sem.at[2, p]) for p in range(CORES)
    ]

    @pl.when(core == home)
    def _():
        for copy in cent_near:
            copy.start()

    def gather_rows(first, second):
        place = iota((cap, lane), 0).astype(F32)
        picks = []
        for l in (first, second):
            base = place + (l * cap).astype(F32)
            picks.append(
                jnp.concatenate(
                    [jnp.where(base == slot_s[b:b + 1, :], 1.0, 0.0).astype(BF16) for b in range(blocks)], axis=1
                )
            )
        pick = jnp.concatenate(picks, axis=0)
        out = dot(pick, emb_s[...]).astype(BF16)
        if not full:
            out = jnp.concatenate([out, dot(pick, jnp.ones((rows, 128), BF16)).astype(BF16)], axis=1)
        return out

    def order(i):
        return lists // 2 + i // 2 - (i % 2) * (2 * (i // 2) + 1)

    def target(j):
        flip = j % quad
        to_member = ((member // 2 + flip // 2) % (quad // 2)) * 2 + (member + flip) % 2
        return (y + j // quad) % planes, to_member

    def row_copy(i):
        to_y, to_member = target(order(i))
        return pltpu.make_async_remote_copy(
            src_ref=send.at[i], dst_ref=recv.at[i], send_sem=p1_send.at[i], recv_sem=p1_recv.at[i],
            device_id={"list": to_y * CORES + core, "shard": group * quad + to_member}, device_id_type=MESH,
        )

    def list_of(i):
        to_y, to_member = target(order(i))
        return to_y * quad + to_member

    def prepare(p):
        found = gather_rows(list_of(2 * p), list_of(2 * p + 1))
        send[2 * p] = found[:cap]
        send[2 * p + 1] = found[cap:]

    def start_rows(p):
        row_copy(2 * p).start()
        row_copy(2 * p + 1).start()

    pairs = lists // 2
    prepare(0)
    pl.semaphore_wait(barrier, in_plane - 1 + (planes - 1) * quad)
    start_rows(0)

    @pl.when(core == home)
    def _():
        for copy in cent_far:
            copy.start()

    def route(p, c):
        prepare(p)
        start_rows(p)
        return c

    def hold(p, c):
        prepare(p)
        return c

    lax.fori_loop(1, AHEAD // 2, route, 0)
    lax.fori_loop(AHEAD // 2, pairs - 1, hold, 0)
    found = gather_rows(list_of(lists - 2), list_of(lists - 1))
    send[lists - 2] = found[:cap]
    recv[lists - 1] = found[cap:]

    @pl.when(core == home)
    def _():
        for copy in cent_near:
            copy.wait()

    @pl.when(core != home)
    def _():
        for copy in cent_far:
            copy.wait_recv()

    def square(i, c):
        at = pl.ds(pl.multiple_of(i * share, share), share)
        some = cbuf[i // halves, i % halves].astype(F32)
        csq[at, :] = jnp.broadcast_to((0.5 * SHARP) * jnp.sum(some * some, axis=1, keepdims=True), (share, cap))
        return c

    lax.fori_loop(0, n_shard, square, 0)

    def block(i, n):
        return recv[pl.ds(i, n), :, :].reshape(n * cap, recv.shape[2])

    def responses(i, n):
        cents = cbuf[...].reshape(fine, width)
        x = block(i, n)[:, :width]
        raw = lax.dot_general(cents, x, (((1,), (1,)), ((), ())), preferred_element_type=F32)
        scores = SHARP * raw - jnp.concatenate([csq[...]] * n, axis=1)
        grown = jnp.exp(scores - jnp.max(scores, axis=0, keepdims=True))
        return (grown * (1.0 / jnp.sum(grown, axis=0, keepdims=True))).astype(BF16)

    def terms(i, n, resp):
        found = block(i, n)
        flags = jnp.ones((n * cap, 128), BF16) if full else found[:, width:]
        return dot(resp, found[:, :width]), dot(resp, flags)

    def add(i, n, at, resp):
        sums, mass = terms(i, n, resp)
        acc[at, :width] += sums
        acc[at, width:] += mass

    sums, mass = terms(lists - 1, 1, responses(lists - 1, 1))
    acc[:, :width] = sums
    acc[:, width:] = mass

    def take(p, c):
        for i in (2 * p, 2 * p + 1):
            row_copy(i).wait_send()

            @pl.when(i + AHEAD < lists - 1)
            def _():
                row_copy(i + AHEAD).start()

        row_copy(2 * p).wait_recv()
        row_copy(2 * p + 1).wait_recv()
        add(2 * p, 2, slice(None), responses(2 * p, 2))
        return c

    lax.fori_loop(0, pairs - 1, take, 0)

    final = lists - 2
    row_copy(final).wait_send()
    row_copy(final).wait_recv()
    resp_s[...] = responses(final, 1)

    def add_last(p, step):
        to_group = (group + 1 + step) % groups
        at = pl.ds(pl.multiple_of(p * half + to_group * per_group * share, share), per_group * share)
        add(final, 1, at, resp_s[at, :])

    eye = iota((share, 128), 0) == iota((share, 128), 1)

    def pair(t):
        return ((group + 1 + t // per_group) % groups) * per_group + (t + sh // CORES) % per_group

    def fine_rows(p, t):
        return pl.ds(pl.multiple_of(p * half + pair(t) * share, share), share)

    def mass_row(at):
        tile = acc[at, width:]
        return jnp.broadcast_to(jnp.sum(jnp.where(eye, tile, 0.0), axis=0, keepdims=True), (8, 128))

    def part_copy(t):
        return pltpu.make_async_remote_copy(
            src_ref=part.at[t], dst_ref=other.at[t], send_sem=part_send.at[t], recv_sem=part_recv.at[t],
            device_id=partner, device_id_type=MESH,
        )

    def mass_copy(t):
        return pltpu.make_async_remote_copy(
            src_ref=mpart.at[t], dst_ref=mother.at[t], send_sem=mp_sem.at[0, t], recv_sem=mp_sem.at[1, t],
            device_id=partner, device_id_type=MESH,
        )

    def give(t, c):
        at = fine_rows(1 - core, t)
        part[t] = acc[at, :width].astype(BF16)
        part_copy(t).start()
        mpart[t] = mass_row(at)
        mass_copy(t).start()
        return c

    def fin_copies(t):
        to = {"list": y * CORES + home, "shard": CORES * pair(t) + core}
        at = hidx * groups + group
        return [
            pltpu.make_async_remote_copy(
                src_ref=src.at[t], dst_ref=dst.at[at], send_sem=ss.at[t], recv_sem=rs.at[at],
                device_id=to, device_id_type=MESH,
            )
            for src, dst, ss, rs in ((merged, fin, fin_send, fin_recv), (mmerged, mfin, mf_send, mf_recv))
        ]

    def own_copies(t):
        at = hidx * groups + group
        return [
            pltpu.make_async_copy(merged.at[t], fin.at[at], fin_recv.at[at]),
            pltpu.make_async_copy(mmerged.at[t], mfin.at[at], mf_recv.at[at]),
        ]

    def is_own(t):
        return (home == core) & (CORES * pair(t) + core == sh)

    def forward(t, c):
        at = fine_rows(core, t)
        part_copy(t).wait_recv()
        mass_copy(t).wait_recv()
        merged[t] = (acc[at, :width] + other[t].astype(F32)).astype(BF16)
        mmerged[t] = mass_row(at) + mother[t]

        @pl.when(is_own(t))
        def _():
            for copy in own_copies(t):
                copy.start()

        @pl.when(jnp.logical_not(is_own(t)))
        def _():
            for copy in fin_copies(t):
                copy.start()

        return c

    def far_step(step, c):
        add_last(1 - core, step)
        lax.fori_loop(step * per_group, (step + 1) * per_group, give, 0)
        add_last(core, step)
        return c

    far = (groups - 1) * per_group
    lax.fori_loop(0, groups - 1, far_step, 0)
    add_last(1 - core, groups - 1)
    lax.fori_loop(far, halves, give, 0)
    lax.fori_loop(0, far, forward, 0)
    add_last(core, groups - 1)
    lax.fori_loop(far, halves, forward, 0)

    @pl.when(core == home)
    def _():
        for copy in cent_far:
            copy.wait_send()

    def sent_parts(t, c):
        part_copy(t).wait_send()
        mass_copy(t).wait_send()
        return c

    lax.fori_loop(0, halves, sent_parts, 0)

    def arrived(i):
        return [
            pltpu.make_async_copy(fin.at[i], fin.at[i], fin_recv.at[i]),
            pltpu.make_async_copy(mfin.at[i], mfin.at[i], mf_recv.at[i]),
        ]

    own_in.wait()
    mass = [jnp.zeros((1, 128), F32) for _ in range(local_lists)]
    for k in range(groups):
        for h in range(local_lists):
            i = h * groups + (group + k) % groups
            for copy in arrived(i):
                copy.wait()
            so_far = own_s[h].astype(F32) * PRIOR if k == 0 else out_ref[h]
            so_far = so_far + fin[i].astype(F32)
            mass[h] = mass[h] + mfin[i, 0:1, :]
            if k == groups - 1:
                column = jnp.sum(jnp.where(eye, mass[h], 0.0), axis=1, keepdims=True)
                so_far = so_far / (column + PRIOR)
            out_ref[h] = so_far

    def sent_fin(t, c):
        @pl.when(jnp.logical_not(is_own(t)))
        def _():
            for copy in fin_copies(t):
                copy.wait_send()

        return c

    lax.fori_loop(0, halves, sent_fin, 0)


def solution(mesh):
    n_list, n_shard = mesh.shape["list"], mesh.shape["shard"]

    def per_device(embeddings, list_ids, centroids):
        rows, width = embeddings.shape
        local_lists, fine, _ = centroids.shape
        cap = rows // 8
        lists = local_lists * n_list
        full = lists * cap == rows
        sent = width if full else width + 128
        share = fine // n_shard
        halves = n_shard // CORES
        arrivals = local_lists * (n_shard // (local_lists * CORES))
        dma = pltpu.SemaphoreType.DMA
        vmem = pl.BlockSpec(memory_space=pltpu.VMEM)
        flops = 2 * rows * lists * cap * width + 4 * lists * cap * fine * width
        return pl.pallas_call(
            functools.partial(kernel, n_list, n_shard, full),
            out_shape=jax.ShapeDtypeStruct((local_lists, share, width), F32),
            in_specs=[vmem, pl.BlockSpec(memory_space=pl.ANY), pl.BlockSpec(memory_space=pl.ANY)],
            out_specs=vmem,
            scratch_shapes=[
                pltpu.VMEM((rows, width), BF16),
                pltpu.VMEM((local_lists, share, width), BF16),
                pltpu.VMEM((fine, cap), BF16),
                pltpu.VMEM((rows // cap, cap), F32),
                pltpu.VMEM((lists, cap, sent), BF16),
                pltpu.VMEM((lists, cap, sent), BF16),
                pltpu.VMEM((CORES, halves, share, width), BF16),
                pltpu.VMEM((fine, cap), F32),
                pltpu.VMEM((fine, width + 128), F32),
                pltpu.VMEM((halves, share, width), BF16),
                pltpu.VMEM((halves, 8, 128), F32),
                pltpu.VMEM((halves, share, width), BF16),
                pltpu.VMEM((halves, 8, 128), F32),
                pltpu.VMEM((halves, share, width), BF16),
                pltpu.VMEM((halves, 8, 128), F32),
                pltpu.VMEM((arrivals, share, width), BF16),
                pltpu.VMEM((arrivals, 8, 128), F32),
                dma((2,)),
                dma((3, CORES)),
                dma((lists,)),
                dma((lists,)),
                dma((halves,)),
                dma((halves,)),
                dma((2, halves)),
                dma((halves,)),
                dma((arrivals,)),
                dma((halves,)),
                dma((arrivals,)),
            ],
            compiler_params=pltpu.CompilerParams(
                collective_id=0, has_side_effects=True, vmem_limit_bytes=52 * 2**20
            ),
            cost_estimate=pl.CostEstimate(
                flops=flops, bytes_accessed=4 * rows * width, transcendentals=lists * cap * fine
            ),
        )(list_ids.T, embeddings, centroids.reshape(local_lists, halves, CORES, share, width))

    placed = (P(("list", "shard"), None), P(("list", "shard"), None), P("list", None, None))
    return jax.shard_map(
        per_device, mesh=mesh, in_specs=placed, out_specs=P("list", "shard", None), check_vma=False
    )
```

```python
import functools

import jax
import jax.numpy as jnp
from jax import lax
from jax.experimental import pallas as pl
from jax.experimental.pallas import tpu as pltpu
from jax.sharding import PartitionSpec as P

SHARP = 0.1
PRIOR = 1.0
MESH = pl.DeviceIdType.MESH
F32 = jnp.float32
BF16 = jnp.bfloat16
CORES = 2
AHEAD = 4


def iota(shape, axis):
    return lax.broadcasted_iota(jnp.int32, shape, axis)


def dot(a, b):
    return jnp.dot(a, b, preferred_element_type=F32)


def kernel(
    n_list, n_shard, full,
    ids_ref, emb_ref, cent_ref, out_ref,
    emb_s, own_s, resp_s, slot_s, send, recv, cbuf, csq, acc,
    part, mpart, other, mother, merged, mmerged, fin, mfin,
    in_sem, cent_sem, p1_send, p1_recv, part_send, part_recv, mp_sem,
    fin_send, fin_recv, mf_send, mf_recv,
):
    local_lists, _, _, share, width = cent_ref.shape
    fine = n_shard * share
    quad = local_lists * CORES
    planes = n_list // CORES
    lists = planes * quad
    groups = n_shard // quad
    halves = n_shard // CORES
    per_group = quad // CORES
    half = halves * share
    rows = emb_ref.shape[0]
    cap = rows // 8
    li, sh = lax.axis_index("list"), lax.axis_index("shard")
    y, core = li // CORES, li % CORES
    group, member = sh // quad, sh % quad
    home, hidx = member // local_lists, member % local_lists
    partner = {"list": y * CORES + (1 - core), "shard": sh}

    emb_in = pltpu.make_async_copy(emb_ref, emb_s, in_sem.at[0])
    own_in = pltpu.make_async_copy(cent_ref.at[:, sh // CORES, sh % CORES], own_s, in_sem.at[1])
    emb_in.start()
    own_in.start()

    barrier = pltpu.get_barrier_semaphore()
    in_plane = CORES * n_shard

    def greet_plane(i, c):
        at = (core * n_shard + sh + i) % in_plane
        pl.semaphore_signal(
            barrier, inc=1, device_id={"list": y * CORES + at // n_shard, "shard": at % n_shard}, device_id_type=MESH
        )
        return c

    def greet_far(i, c):
        to_y = (y + 1 + i // quad) % planes
        pl.semaphore_signal(
            barrier, inc=1, device_id={"list": to_y * CORES + core, "shard": group * quad + i % quad}, device_id_type=MESH
        )
        return c

    lax.fori_loop(1, in_plane, greet_plane, 0)
    lax.fori_loop(0, (planes - 1) * quad, greet_far, 0)

    blocks, lane = rows // cap, cap
    ids = jnp.concatenate([ids_ref[:, b * lane:(b + 1) * lane] for b in range(blocks)], axis=0)
    hot = [jnp.where(ids == l, 1.0, 0.0).astype(F32) for l in range(lists)]
    hots = jnp.concatenate(hot, axis=0).astype(BF16)
    many = lists * blocks
    before = jnp.where(iota((lane, lane), 0) < iota((lane, lane), 1), 1.0, 0.0).astype(BF16)
    rank = dot(hots, before)
    totals = dot(hots, jnp.ones((lane, lane), BF16)).astype(BF16)
    up, down = iota((many, many), 0), iota((many, many), 1)
    earlier = jnp.where((up // blocks == down // blocks) & (down < up), 1.0, 0.0).astype(BF16)
    rank = rank + dot(earlier, totals)
    slot = jnp.zeros((blocks, lane), F32)
    for l in range(lists):
        slot = slot + hot[l] * (rank[l * blocks:(l + 1) * blocks] + float(l * cap))
    slot_s[...] = slot

    emb_in.wait()

    cent_far = [
        pltpu.make_async_remote_copy(
            src_ref=cent_ref.at[hidx, :, p], dst_ref=cbuf.at[p], send_sem=cent_sem.at[0, p], recv_sem=cent_sem.at[1, p],
            device_id=partner, device_id_type=MESH,
        )
        for p in range(CORES)
    ]
    cent_near = [
        pltpu.make_async_copy(cent_ref.at[hidx, :, p], cbuf.at[p], cent_sem.at[2, p]) for p in range(CORES)
    ]

    @pl.when(core == home)
    def _():
        for copy in cent_near:
            copy.start()

    def gather_rows(*wanted):
        place = iota((cap, lane), 0).astype(F32)
        picks = []
        for l in wanted:
            base = place + (l * cap).astype(F32)
            picks.append(
                jnp.concatenate(
                    [jnp.where(base == slot_s[b:b + 1, :], 1.0, 0.0).astype(BF16) for b in range(blocks)], axis=1
                )
            )
        pick = jnp.concatenate(picks, axis=0)
        out = dot(pick, emb_s[...]).astype(BF16)
        if not full:
            out = jnp.concatenate([out, dot(pick, jnp.ones((rows, 128), BF16)).astype(BF16)], axis=1)
        return out

    def order(i):
        return lists // 2 + i // 2 - (i % 2) * (2 * (i // 2) + 1)

    def target(j):
        flip = j % quad
        to_member = ((member // 2 + flip // 2) % (quad // 2)) * 2 + (member + flip) % 2
        return (y + j // quad) % planes, to_member

    def row_copy(i):
        to_y, to_member = target(order(i))
        return pltpu.make_async_remote_copy(
            src_ref=send.at[i], dst_ref=recv.at[i], send_sem=p1_send.at[i], recv_sem=p1_recv.at[i],
            device_id={"list": to_y * CORES + core, "shard": group * quad + to_member}, device_id_type=MESH,
        )

    def list_of(i):
        to_y, to_member = target(order(i))
        return to_y * quad + to_member

    def prepare(p):
        found = gather_rows(list_of(2 * p), list_of(2 * p + 1))
        send[2 * p] = found[:cap]
        send[2 * p + 1] = found[cap:]

    def start_rows(p):
        row_copy(2 * p).start()
        row_copy(2 * p + 1).start()

    pairs = lists // 2
    send[0] = gather_rows(list_of(0))
    pl.semaphore_wait(barrier, in_plane - 1 + (planes - 1) * quad)
    row_copy(0).start()
    send[1] = gather_rows(list_of(1))
    row_copy(1).start()

    @pl.when(core == home)
    def _():
        for copy in cent_far:
            copy.start()

    def route(p, c):
        prepare(p)
        start_rows(p)
        return c

    def hold(p, c):
        prepare(p)
        return c

    lax.fori_loop(1, AHEAD // 2, route, 0)
    lax.fori_loop(AHEAD // 2, pairs - 1, hold, 0)
    found = gather_rows(list_of(lists - 2), list_of(lists - 1))
    send[lists - 2] = found[:cap]
    recv[lists - 1] = found[cap:]

    @pl.when(core == home)
    def _():
        for copy in cent_near:
            copy.wait()

    @pl.when(core != home)
    def _():
        for copy in cent_far:
            copy.wait_recv()

    def square(i, c):
        at = pl.ds(pl.multiple_of(i * share, share), share)
        some = cbuf[i // halves, i % halves].astype(F32)
        csq[at, :] = jnp.broadcast_to((0.5 * SHARP) * jnp.sum(some * some, axis=1, keepdims=True), (share, cap))
        return c

    lax.fori_loop(0, n_shard, square, 0)

    def block(i, n):
        return recv[pl.ds(i, n), :, :].reshape(n * cap, recv.shape[2])

    def responses(i, n):
        cents = cbuf[...].reshape(fine, width)
        x = block(i, n)[:, :width]
        raw = lax.dot_general(cents, x, (((1,), (1,)), ((), ())), preferred_element_type=F32)
        scores = SHARP * raw - jnp.concatenate([csq[...]] * n, axis=1)
        grown = jnp.exp(scores - jnp.max(scores, axis=0, keepdims=True))
        return (grown * (1.0 / jnp.sum(grown, axis=0, keepdims=True))).astype(BF16)

    def terms(i, n, resp):
        found = block(i, n)
        flags = jnp.ones((n * cap, 128), BF16) if full else found[:, width:]
        return dot(resp, found[:, :width]), dot(resp, flags)

    def add(i, n, at, resp):
        sums, mass = terms(i, n, resp)
        acc[at, :width] += sums
        acc[at, width:] += mass

    sums, mass = terms(lists - 1, 1, responses(lists - 1, 1))
    acc[:, :width] = sums
    acc[:, width:] = mass

    def take(p, c):
        for i in (2 * p, 2 * p + 1):
            row_copy(i).wait_send()

            @pl.when(i + AHEAD < lists - 1)
            def _():
                row_copy(i + AHEAD).start()

        row_copy(2 * p).wait_recv()
        row_copy(2 * p + 1).wait_recv()
        add(2 * p, 2, slice(None), responses(2 * p, 2))
        return c

    def take_one(i, c):
        row_copy(i).wait_send()
        row_copy(i).wait_recv()
        add(i, 1, slice(None), responses(i, 1))
        return c

    lax.fori_loop(0, pairs - 2, take, 0)
    lax.fori_loop(lists - 4, lists - 2, take_one, 0)

    final = lists - 2
    row_copy(final).wait_send()
    row_copy(final).wait_recv()
    resp_s[...] = responses(final, 1)

    def add_last(p, step):
        to_group = (group + 1 + step) % groups
        at = pl.ds(pl.multiple_of(p * half + to_group * per_group * share, share), per_group * share)
        add(final, 1, at, resp_s[at, :])

    eye = iota((share, 128), 0) == iota((share, 128), 1)

    def pair(t):
        return ((group + 1 + t // per_group) % groups) * per_group + (t + sh // CORES) % per_group

    def fine_rows(p, t):
        return pl.ds(pl.multiple_of(p * half + pair(t) * share, share), share)

    def mass_row(at):
        tile = acc[at, width:]
        return jnp.broadcast_to(jnp.sum(jnp.where(eye, tile, 0.0), axis=0, keepdims=True), (8, 128))

    def part_copy(t):
        return pltpu.make_async_remote_copy(
            src_ref=part.at[t], dst_ref=other.at[t], send_sem=part_send.at[t], recv_sem=part_recv.at[t],
            device_id=partner, device_id_type=MESH,
        )

    def mass_copy(t):
        return pltpu.make_async_remote_copy(
            src_ref=mpart.at[t], dst_ref=mother.at[t], send_sem=mp_sem.at[0, t], recv_sem=mp_sem.at[1, t],
            device_id=partner, device_id_type=MESH,
        )

    def give(t, c):
        at = fine_rows(1 - core, t)
        part[t] = acc[at, :width].astype(BF16)
        part_copy(t).start()
        mpart[t] = mass_row(at)
        mass_copy(t).start()
        return c

    def fin_copies(t):
        to = {"list": y * CORES + home, "shard": CORES * pair(t) + core}
        at = hidx * groups + group
        return [
            pltpu.make_async_remote_copy(
                src_ref=src.at[t], dst_ref=dst.at[at], send_sem=ss.at[t], recv_sem=rs.at[at],
                device_id=to, device_id_type=MESH,
            )
            for src, dst, ss, rs in ((merged, fin, fin_send, fin_recv), (mmerged, mfin, mf_send, mf_recv))
        ]

    def own_copies(t):
        at = hidx * groups + group
        return [
            pltpu.make_async_copy(merged.at[t], fin.at[at], fin_recv.at[at]),
            pltpu.make_async_copy(mmerged.at[t], mfin.at[at], mf_recv.at[at]),
        ]

    def is_own(t):
        return (home == core) & (CORES * pair(t) + core == sh)

    def forward(t, c):
        at = fine_rows(core, t)
        part_copy(t).wait_recv()
        mass_copy(t).wait_recv()
        merged[t] = (acc[at, :width] + other[t].astype(F32)).astype(BF16)
        mmerged[t] = mass_row(at) + mother[t]

        @pl.when(is_own(t))
        def _():
            for copy in own_copies(t):
                copy.start()

        @pl.when(jnp.logical_not(is_own(t)))
        def _():
            for copy in fin_copies(t):
                copy.start()

        return c

    def far_step(step, c):
        add_last(1 - core, step)
        lax.fori_loop(step * per_group, (step + 1) * per_group, give, 0)
        add_last(core, step)
        return c

    far = (groups - 1) * per_group
    lax.fori_loop(0, groups - 1, far_step, 0)
    add_last(1 - core, groups - 1)
    lax.fori_loop(far, halves, give, 0)
    lax.fori_loop(0, far, forward, 0)
    add_last(core, groups - 1)
    lax.fori_loop(far, halves, forward, 0)

    @pl.when(core == home)
    def _():
        for copy in cent_far:
            copy.wait_send()

    def sent_parts(t, c):
        part_copy(t).wait_send()
        mass_copy(t).wait_send()
        return c

    lax.fori_loop(0, halves, sent_parts, 0)

    def arrived(i):
        return [
            pltpu.make_async_copy(fin.at[i], fin.at[i], fin_recv.at[i]),
            pltpu.make_async_copy(mfin.at[i], mfin.at[i], mf_recv.at[i]),
        ]

    own_in.wait()
    mass = [jnp.zeros((1, 128), F32) for _ in range(local_lists)]
    for k in range(groups):
        for h in range(local_lists):
            i = h * groups + (group + k) % groups
            for copy in arrived(i):
                copy.wait()
            so_far = own_s[h].astype(F32) * PRIOR if k == 0 else out_ref[h]
            so_far = so_far + fin[i].astype(F32)
            mass[h] = mass[h] + mfin[i, 0:1, :]
            if k == groups - 1:
                column = jnp.sum(jnp.where(eye, mass[h], 0.0), axis=1, keepdims=True)
                so_far = so_far / (column + PRIOR)
            out_ref[h] = so_far

    def sent_fin(t, c):
        @pl.when(jnp.logical_not(is_own(t)))
        def _():
            for copy in fin_copies(t):
                copy.wait_send()

        return c

    lax.fori_loop(0, halves, sent_fin, 0)


def solution(mesh):
    n_list, n_shard = mesh.shape["list"], mesh.shape["shard"]

    def per_device(embeddings, list_ids, centroids):
        rows, width = embeddings.shape
        local_lists, fine, _ = centroids.shape
        cap = rows // 8
        lists = local_lists * n_list
        full = lists * cap == rows
        sent = width if full else width + 128
        share = fine // n_shard
        halves = n_shard // CORES
        arrivals = local_lists * (n_shard // (local_lists * CORES))
        dma = pltpu.SemaphoreType.DMA
        vmem = pl.BlockSpec(memory_space=pltpu.VMEM)
        flops = 2 * rows * lists * cap * width + 4 * lists * cap * fine * width
        return pl.pallas_call(
            functools.partial(kernel, n_list, n_shard, full),
            out_shape=jax.ShapeDtypeStruct((local_lists, share, width), F32),
            in_specs=[vmem, pl.BlockSpec(memory_space=pl.ANY), pl.BlockSpec(memory_space=pl.ANY)],
            out_specs=vmem,
            scratch_shapes=[
                pltpu.VMEM((rows, width), BF16),
                pltpu.VMEM((local_lists, share, width), BF16),
                pltpu.VMEM((fine, cap), BF16),
                pltpu.VMEM((rows // cap, cap), F32),
                pltpu.VMEM((lists, cap, sent), BF16),
                pltpu.VMEM((lists, cap, sent), BF16),
                pltpu.VMEM((CORES, halves, share, width), BF16),
                pltpu.VMEM((fine, cap), F32),
                pltpu.VMEM((fine, width + 128), F32),
                pltpu.VMEM((halves, share, width), BF16),
                pltpu.VMEM((halves, 8, 128), F32),
                pltpu.VMEM((halves, share, width), BF16),
                pltpu.VMEM((halves, 8, 128), F32),
                pltpu.VMEM((halves, share, width), BF16),
                pltpu.VMEM((halves, 8, 128), F32),
                pltpu.VMEM((arrivals, share, width), BF16),
                pltpu.VMEM((arrivals, 8, 128), F32),
                dma((2,)),
                dma((3, CORES)),
                dma((lists,)),
                dma((lists,)),
                dma((halves,)),
                dma((halves,)),
                dma((2, halves)),
                dma((halves,)),
                dma((arrivals,)),
                dma((halves,)),
                dma((arrivals,)),
            ],
            compiler_params=pltpu.CompilerParams(
                collective_id=0, has_side_effects=True, vmem_limit_bytes=52 * 2**20
            ),
            cost_estimate=pl.CostEstimate(
                flops=flops, bytes_accessed=4 * rows * width, transcendentals=lists * cap * fine
            ),
        )(list_ids.T, embeddings, centroids.reshape(local_lists, halves, CORES, share, width))

    placed = (P(("list", "shard"), None), P(("list", "shard"), None), P("list", None, None))
    return jax.shard_map(
        per_device, mesh=mesh, in_specs=placed, out_specs=P("list", "shard", None), check_vma=False
    )
```

```python
import functools

import jax
import jax.numpy as jnp
from jax import lax
from jax.experimental import pallas as pl
from jax.experimental.pallas import tpu as pltpu
from jax.sharding import PartitionSpec as P

SHARP = 0.1
PRIOR = 1.0
MESH = pl.DeviceIdType.MESH
F32 = jnp.float32
BF16 = jnp.bfloat16
CORES = 2
AHEAD = 7


def iota(shape, axis):
    return lax.broadcasted_iota(jnp.int32, shape, axis)


def dot(a, b):
    return jnp.dot(a, b, preferred_element_type=F32)


def kernel(
    n_list, n_shard, full,
    ids_ref, emb_ref, cent_ref, out_ref,
    emb_s, own_s, resp_s, slot_s, send, recv, cbuf, csq, acc,
    part, mpart, other, mother, merged, mmerged, fin, mfin,
    in_sem, cent_sem, p1_send, p1_recv, part_send, part_recv, mp_sem,
    fin_send, fin_recv, mf_send, mf_recv,
):
    local_lists, _, _, share, width = cent_ref.shape
    fine = n_shard * share
    quad = local_lists * CORES
    planes = n_list // CORES
    lists = planes * quad
    groups = n_shard // quad
    halves = n_shard // CORES
    per_group = quad // CORES
    half = halves * share
    rows = emb_ref.shape[0]
    cap = rows // 8
    li, sh = lax.axis_index("list"), lax.axis_index("shard")
    y, core = li // CORES, li % CORES
    group, member = sh // quad, sh % quad
    home, hidx = member // local_lists, member % local_lists
    partner = {"list": y * CORES + (1 - core), "shard": sh}

    emb_in = pltpu.make_async_copy(emb_ref, emb_s, in_sem.at[0])
    own_in = pltpu.make_async_copy(cent_ref.at[:, sh // CORES, sh % CORES], own_s, in_sem.at[1])
    emb_in.start()
    own_in.start()

    barrier = pltpu.get_barrier_semaphore()
    in_plane = CORES * n_shard

    def greet_plane(i, c):
        at = (core * n_shard + sh + i) % in_plane
        pl.semaphore_signal(
            barrier, inc=1, device_id={"list": y * CORES + at // n_shard, "shard": at % n_shard}, device_id_type=MESH
        )
        return c

    def greet_far(i, c):
        to_y = (y + 1 + i // quad) % planes
        pl.semaphore_signal(
            barrier, inc=1, device_id={"list": to_y * CORES + core, "shard": group * quad + i % quad}, device_id_type=MESH
        )
        return c

    lax.fori_loop(1, in_plane, greet_plane, 0)
    lax.fori_loop(0, (planes - 1) * quad, greet_far, 0)

    blocks, lane = rows // cap, cap
    ids = jnp.concatenate([ids_ref[:, b * lane:(b + 1) * lane] for b in range(blocks)], axis=0)
    hot = [jnp.where(ids == l, 1.0, 0.0).astype(F32) for l in range(lists)]
    hots = jnp.concatenate(hot, axis=0).astype(BF16)
    many = lists * blocks
    before = jnp.where(iota((lane, lane), 0) < iota((lane, lane), 1), 1.0, 0.0).astype(BF16)
    rank = dot(hots, before)
    totals = dot(hots, jnp.ones((lane, lane), BF16)).astype(BF16)
    up, down = iota((many, many), 0), iota((many, many), 1)
    earlier = jnp.where((up // blocks == down // blocks) & (down < up), 1.0, 0.0).astype(BF16)
    rank = rank + dot(earlier, totals)
    slot = jnp.zeros((blocks, lane), F32)
    for l in range(lists):
        slot = slot + hot[l] * (rank[l * blocks:(l + 1) * blocks] + float(l * cap))
    slot_s[...] = slot

    emb_in.wait()
    pl.semaphore_wait(barrier, in_plane - 1 + (planes - 1) * quad)

    cent_far = [
        pltpu.make_async_remote_copy(
            src_ref=cent_ref.at[hidx, :, p], dst_ref=cbuf.at[p], send_sem=cent_sem.at[0, p], recv_sem=cent_sem.at[1, p],
            device_id=partner, device_id_type=MESH,
        )
        for p in range(CORES)
    ]
    cent_near = [
        pltpu.make_async_copy(cent_ref.at[hidx, :, p], cbuf.at[p], cent_sem.at[2, p]) for p in range(CORES)
    ]

    @pl.when(core == home)
    def _():
        for copy in cent_far + cent_near:
            copy.start()

    def gather_rows(l, dst):
        base = (l * cap).astype(F32)
        place = iota((cap, lane), 0).astype(F32) + base
        pick = jnp.concatenate(
            [jnp.where(place == slot_s[b:b + 1, :], 1.0, 0.0).astype(BF16) for b in range(blocks)], axis=1
        )
        dst[:, :width] = dot(pick, emb_s[...]).astype(BF16)
        if not full:
            dst[:, width:] = dot(pick, jnp.ones((rows, 128), BF16)).astype(BF16)

    def order(i):
        return lists // 2 + i // 2 - (i % 2) * (2 * (i // 2) + 1)

    def target(j):
        flip = j % quad
        to_member = ((member // 2 + flip // 2) % (quad // 2)) * 2 + (member + flip) % 2
        return (y + j // quad) % planes, to_member

    def row_copy(j):
        to_y, to_member = target(j)
        return pltpu.make_async_remote_copy(
            src_ref=send.at[j], dst_ref=recv.at[j], send_sem=p1_send.at[j], recv_sem=p1_recv.at[j],
            device_id={"list": to_y * CORES + core, "shard": group * quad + to_member}, device_id_type=MESH,
        )

    def prepare(i):
        to_y, to_member = target(order(i))
        gather_rows(to_y * quad + to_member, send.at[order(i)])

    def route(i, c):
        prepare(i)
        row_copy(order(i)).start()
        return c

    def hold(i, c):
        prepare(i)
        return c

    lax.fori_loop(0, AHEAD, route, 0)
    lax.fori_loop(AHEAD, lists - 1, hold, 0)
    gather_rows(y * quad + member, recv.at[0])

    @pl.when(core == home)
    def _():
        for copy in cent_near:
            copy.wait()

    @pl.when(core != home)
    def _():
        for copy in cent_far:
            copy.wait_recv()

    def square(i, c):
        at = pl.ds(pl.multiple_of(i * share, share), share)
        some = cbuf[i // halves, i % halves].astype(F32)
        csq[at, :] = jnp.broadcast_to((0.5 * SHARP) * jnp.sum(some * some, axis=1, keepdims=True), (share, cap))
        return c

    lax.fori_loop(0, n_shard, square, 0)
    acc[...] = jnp.zeros_like(acc)

    def responses(j):
        cents = cbuf[...].reshape(fine, width)
        raw = lax.dot_general(
            cents, recv[j, :, :width], (((1,), (1,)), ((), ())), preferred_element_type=F32
        )
        scores = SHARP * raw - csq[...]
        grown = jnp.exp(scores - jnp.max(scores, axis=0, keepdims=True))
        return (grown * (1.0 / jnp.sum(grown, axis=0, keepdims=True))).astype(BF16)

    def add(j, at, resp):
        acc[at, :width] += dot(resp, recv[j, :, :width])
        acc[at, width:] += dot(resp, jnp.ones((cap, 128), BF16) if full else recv[j, :, width:])

    add(0, slice(None), responses(0))

    def await_rows(i):
        row_copy(order(i)).wait_send()

        @pl.when(i + AHEAD < lists - 1)
        def _():
            row_copy(order(i + AHEAD)).start()

        row_copy(order(i)).wait_recv()

    def take(i, c):
        await_rows(i)
        add(order(i), slice(None), responses(order(i)))
        return c

    lax.fori_loop(0, lists - 2, take, 0)

    final = lists - 2
    await_rows(final)
    resp_s[...] = responses(order(final))

    def add_last(p):
        at = pl.ds(pl.multiple_of(p * half, half), half)
        add(order(final), at, resp_s[at, :])

    add_last(1 - core)

    eye = iota((share, 128), 0) == iota((share, 128), 1)

    def pair(t):
        return ((group + 1 + t // per_group) % groups) * per_group + (t + sh // CORES) % per_group

    def fine_rows(p, t):
        return pl.ds(pl.multiple_of(p * half + pair(t) * share, share), share)

    def mass_row(at):
        tile = acc[at, width:]
        return jnp.broadcast_to(jnp.sum(jnp.where(eye, tile, 0.0), axis=0, keepdims=True), (8, 128))

    def part_copy(t):
        return pltpu.make_async_remote_copy(
            src_ref=part.at[t], dst_ref=other.at[t], send_sem=part_send.at[t], recv_sem=part_recv.at[t],
            device_id=partner, device_id_type=MESH,
        )

    mass_copy = pltpu.make_async_remote_copy(
        src_ref=mpart, dst_ref=mother, send_sem=mp_sem.at[0], recv_sem=mp_sem.at[1],
        device_id=partner, device_id_type=MESH,
    )

    def give(t, c):
        at = fine_rows(1 - core, t)
        part[t] = acc[at, :width].astype(BF16)
        part_copy(t).start()
        mpart[t] = mass_row(at)
        return c

    lax.fori_loop(0, halves, give, 0)
    mass_copy.start()
    add_last(core)

    def fin_copies(t):
        to = {"list": y * CORES + home, "shard": CORES * pair(t) + core}
        at = hidx * groups + group
        return [
            pltpu.make_async_remote_copy(
                src_ref=src.at[t], dst_ref=dst.at[at], send_sem=ss.at[t], recv_sem=rs.at[at],
                device_id=to, device_id_type=MESH,
            )
            for src, dst, ss, rs in ((merged, fin, fin_send, fin_recv), (mmerged, mfin, mf_send, mf_recv))
        ]

    def own_copies(t):
        at = hidx * groups + group
        return [
            pltpu.make_async_copy(merged.at[t], fin.at[at], fin_recv.at[at]),
            pltpu.make_async_copy(mmerged.at[t], mfin.at[at], mf_recv.at[at]),
        ]

    def is_own(t):
        return (home == core) & (CORES * pair(t) + core == sh)

    mass_copy.wait_recv()

    def forward(t, c):
        at = fine_rows(core, t)
        part_copy(t).wait_recv()
        merged[t] = (acc[at, :width] + other[t].astype(F32)).astype(BF16)
        mmerged[t] = mass_row(at) + mother[t]

        @pl.when(is_own(t))
        def _():
            for copy in own_copies(t):
                copy.start()

        @pl.when(jnp.logical_not(is_own(t)))
        def _():
            for copy in fin_copies(t):
                copy.start()

        return c

    lax.fori_loop(0, halves, forward, 0)

    @pl.when(core == home)
    def _():
        for copy in cent_far:
            copy.wait_send()

    def sent_parts(t, c):
        part_copy(t).wait_send()
        return c

    lax.fori_loop(0, halves, sent_parts, 0)
    mass_copy.wait_send()

    def arrived(i):
        return [
            pltpu.make_async_copy(fin.at[i], fin.at[i], fin_recv.at[i]),
            pltpu.make_async_copy(mfin.at[i], mfin.at[i], mf_recv.at[i]),
        ]

    own_in.wait()
    for h in range(local_lists):
        sums = own_s[h].astype(F32) * PRIOR
        mass = jnp.zeros((1, 128), F32)
        for k in range(groups):
            i = h * groups + k
            for copy in arrived(i):
                copy.wait()
            sums = sums + fin[i].astype(F32)
            mass = mass + mfin[i, 0:1, :]
        column = jnp.sum(jnp.where(eye, mass, 0.0), axis=1, keepdims=True)
        out_ref[h] = sums / (column + PRIOR)

    def sent_fin(t, c):
        @pl.when(jnp.logical_not(is_own(t)))
        def _():
            for copy in fin_copies(t):
                copy.wait_send()

        return c

    lax.fori_loop(0, halves, sent_fin, 0)


def solution(mesh):
    n_list, n_shard = mesh.shape["list"], mesh.shape["shard"]

    def per_device(embeddings, list_ids, centroids):
        rows, width = embeddings.shape
        local_lists, fine, _ = centroids.shape
        cap = rows // 8
        lists = local_lists * n_list
        full = lists * cap == rows
        sent = width if full else width + 128
        share = fine // n_shard
        halves = n_shard // CORES
        arrivals = local_lists * (n_shard // (local_lists * CORES))
        dma = pltpu.SemaphoreType.DMA
        vmem = pl.BlockSpec(memory_space=pltpu.VMEM)
        flops = 2 * rows * lists * cap * width + 4 * lists * cap * fine * width
        return pl.pallas_call(
            functools.partial(kernel, n_list, n_shard, full),
            out_shape=jax.ShapeDtypeStruct((local_lists, share, width), F32),
            in_specs=[vmem, pl.BlockSpec(memory_space=pl.ANY), pl.BlockSpec(memory_space=pl.ANY)],
            out_specs=vmem,
            scratch_shapes=[
                pltpu.VMEM((rows, width), BF16),
                pltpu.VMEM((local_lists, share, width), BF16),
                pltpu.VMEM((fine, cap), BF16),
                pltpu.VMEM((rows // cap, cap), F32),
                pltpu.VMEM((lists, cap, sent), BF16),
                pltpu.VMEM((lists, cap, sent), BF16),
                pltpu.VMEM((CORES, halves, share, width), BF16),
                pltpu.VMEM((fine, cap), F32),
                pltpu.VMEM((fine, width + 128), F32),
                pltpu.VMEM((halves, share, width), BF16),
                pltpu.VMEM((halves, 8, 128), F32),
                pltpu.VMEM((halves, share, width), BF16),
                pltpu.VMEM((halves, 8, 128), F32),
                pltpu.VMEM((halves, share, width), BF16),
                pltpu.VMEM((halves, 8, 128), F32),
                pltpu.VMEM((arrivals, share, width), BF16),
                pltpu.VMEM((arrivals, 8, 128), F32),
                dma((2,)),
                dma((3, CORES)),
                dma((lists,)),
                dma((lists,)),
                dma((halves,)),
                dma((halves,)),
                dma((2,)),
                dma((halves,)),
                dma((arrivals,)),
                dma((halves,)),
                dma((arrivals,)),
            ],
            compiler_params=pltpu.CompilerParams(
                collective_id=0, has_side_effects=True, vmem_limit_bytes=52 * 2**20
            ),
            cost_estimate=pl.CostEstimate(
                flops=flops, bytes_accessed=4 * rows * width, transcendentals=lists * cap * fine
            ),
        )(list_ids.T, embeddings, centroids.reshape(local_lists, halves, CORES, share, width))

    placed = (P(("list", "shard"), None), P(("list", "shard"), None), P("list", None, None))
    return jax.shard_map(
        per_device, mesh=mesh, in_specs=placed, out_specs=P("list", "shard", None), check_vma=False
    )
```

```python
import functools

import jax
import jax.numpy as jnp
from jax import lax
from jax.experimental import pallas as pl
from jax.experimental.pallas import tpu as pltpu
from jax.sharding import PartitionSpec as P

SHARP = 0.1
PRIOR = 1.0
MESH = pl.DeviceIdType.MESH
F32 = jnp.float32
BF16 = jnp.bfloat16
CORES = 2
AHEAD = 4


def iota(shape, axis):
    return lax.broadcasted_iota(jnp.int32, shape, axis)


def dot(a, b):
    return jnp.dot(a, b, preferred_element_type=F32)


def kernel(
    n_list, n_shard, full,
    ids_ref, emb_ref, cent_ref, out_ref,
    emb_s, own_s, resp_s, slot_s, send, recv, cbuf, csq, acc,
    part, mpart, other, mother, merged, mmerged, fin, mfin,
    in_sem, cent_sem, p1_send, p1_recv, part_send, part_recv, mp_sem,
    fin_send, fin_recv, mf_send, mf_recv,
):
    local_lists, _, _, share, width = cent_ref.shape
    fine = n_shard * share
    quad = local_lists * CORES
    planes = n_list // CORES
    lists = planes * quad
    groups = n_shard // quad
    halves = n_shard // CORES
    per_group = quad // CORES
    half = halves * share
    rows = emb_ref.shape[0]
    cap = rows // 8
    li, sh = lax.axis_index("list"), lax.axis_index("shard")
    y, core = li // CORES, li % CORES
    group, member = sh // quad, sh % quad
    home, hidx = member // local_lists, member % local_lists
    partner = {"list": y * CORES + (1 - core), "shard": sh}

    emb_in = pltpu.make_async_copy(emb_ref, emb_s, in_sem.at[0])
    own_in = pltpu.make_async_copy(cent_ref.at[:, sh // CORES, sh % CORES], own_s, in_sem.at[1])
    emb_in.start()
    own_in.start()

    barrier = pltpu.get_barrier_semaphore()
    in_plane = CORES * n_shard

    def greet_plane(i, c):
        at = (core * n_shard + sh + i) % in_plane
        pl.semaphore_signal(
            barrier, inc=1, device_id={"list": y * CORES + at // n_shard, "shard": at % n_shard}, device_id_type=MESH
        )
        return c

    def greet_far(i, c):
        to_y = (y + 1 + i // quad) % planes
        pl.semaphore_signal(
            barrier, inc=1, device_id={"list": to_y * CORES + core, "shard": group * quad + i % quad}, device_id_type=MESH
        )
        return c

    lax.fori_loop(1, in_plane, greet_plane, 0)
    lax.fori_loop(0, (planes - 1) * quad, greet_far, 0)

    blocks, lane = rows // cap, cap
    ids = jnp.concatenate([ids_ref[:, b * lane:(b + 1) * lane] for b in range(blocks)], axis=0)
    hot = [jnp.where(ids == l, 1.0, 0.0).astype(F32) for l in range(lists)]
    hots = jnp.concatenate(hot, axis=0).astype(BF16)
    many = lists * blocks
    before = jnp.where(iota((lane, lane), 0) < iota((lane, lane), 1), 1.0, 0.0).astype(BF16)
    rank = dot(hots, before)
    totals = dot(hots, jnp.ones((lane, lane), BF16)).astype(BF16)
    up, down = iota((many, many), 0), iota((many, many), 1)
    earlier = jnp.where((up // blocks == down // blocks) & (down < up), 1.0, 0.0).astype(BF16)
    rank = rank + dot(earlier, totals)
    slot = jnp.zeros((blocks, lane), F32)
    for l in range(lists):
        slot = slot + hot[l] * (rank[l * blocks:(l + 1) * blocks] + float(l * cap))
    slot_s[...] = slot

    emb_in.wait()

    cent_far = [
        pltpu.make_async_remote_copy(
            src_ref=cent_ref.at[hidx, :, p], dst_ref=cbuf.at[p], send_sem=cent_sem.at[0, p], recv_sem=cent_sem.at[1, p],
            device_id=partner, device_id_type=MESH,
        )
        for p in range(CORES)
    ]
    cent_near = [
        pltpu.make_async_copy(cent_ref.at[hidx, :, p], cbuf.at[p], cent_sem.at[2, p]) for p in range(CORES)
    ]

    def gather_rows(l, dst):
        base = (l * cap).astype(F32)
        place = iota((cap, lane), 0).astype(F32) + base
        pick = jnp.concatenate(
            [jnp.where(place == slot_s[b:b + 1, :], 1.0, 0.0).astype(BF16) for b in range(blocks)], axis=1
        )
        dst[:, :width] = dot(pick, emb_s[...]).astype(BF16)
        if not full:
            dst[:, width:] = dot(pick, jnp.ones((rows, 128), BF16)).astype(BF16)

    def order(i):
        return lists // 2 + i // 2 - (i % 2) * (2 * (i // 2) + 1)

    def target(j):
        flip = j % quad
        to_member = ((member // 2 + flip // 2) % (quad // 2)) * 2 + (member + flip) % 2
        return (y + j // quad) % planes, to_member

    def row_copy(j):
        to_y, to_member = target(j)
        return pltpu.make_async_remote_copy(
            src_ref=send.at[j], dst_ref=recv.at[j], send_sem=p1_send.at[j], recv_sem=p1_recv.at[j],
            device_id={"list": to_y * CORES + core, "shard": group * quad + to_member}, device_id_type=MESH,
        )

    def prepare(i):
        to_y, to_member = target(order(i))
        gather_rows(to_y * quad + to_member, send.at[order(i)])

    def route(i, c):
        prepare(i)
        row_copy(order(i)).start()
        return c

    def hold(i, c):
        prepare(i)
        return c

    prepare(0)
    pl.semaphore_wait(barrier, in_plane - 1 + (planes - 1) * quad)
    row_copy(order(0)).start()

    @pl.when(core == home)
    def _():
        for copy in cent_far + cent_near:
            copy.start()

    lax.fori_loop(1, AHEAD, route, 0)
    lax.fori_loop(AHEAD, lists - 1, hold, 0)
    gather_rows(y * quad + member, recv.at[0])

    @pl.when(core == home)
    def _():
        for copy in cent_near:
            copy.wait()

    @pl.when(core != home)
    def _():
        for copy in cent_far:
            copy.wait_recv()

    def square(i, c):
        at = pl.ds(pl.multiple_of(i * share, share), share)
        some = cbuf[i // halves, i % halves].astype(F32)
        csq[at, :] = jnp.broadcast_to((0.5 * SHARP) * jnp.sum(some * some, axis=1, keepdims=True), (share, cap))
        return c

    lax.fori_loop(0, n_shard, square, 0)
    acc[...] = jnp.zeros_like(acc)

    def responses(j):
        cents = cbuf[...].reshape(fine, width)
        raw = lax.dot_general(
            cents, recv[j, :, :width], (((1,), (1,)), ((), ())), preferred_element_type=F32
        )
        scores = SHARP * raw - csq[...]
        grown = jnp.exp(scores - jnp.max(scores, axis=0, keepdims=True))
        return (grown * (1.0 / jnp.sum(grown, axis=0, keepdims=True))).astype(BF16)

    def add(j, at, resp):
        acc[at, :width] += dot(resp, recv[j, :, :width])
        acc[at, width:] += dot(resp, jnp.ones((cap, 128), BF16) if full else recv[j, :, width:])

    add(0, slice(None), responses(0))

    def await_rows(i):
        row_copy(order(i)).wait_send()

        @pl.when(i + AHEAD < lists - 1)
        def _():
            row_copy(order(i + AHEAD)).start()

        row_copy(order(i)).wait_recv()

    def take(i, c):
        await_rows(i)
        add(order(i), slice(None), responses(order(i)))
        return c

    lax.fori_loop(0, lists - 2, take, 0)

    final = lists - 2
    await_rows(final)
    resp_s[...] = responses(order(final))

    def add_last(p):
        at = pl.ds(pl.multiple_of(p * half, half), half)
        add(order(final), at, resp_s[at, :])

    add_last(1 - core)

    eye = iota((share, 128), 0) == iota((share, 128), 1)

    def pair(t):
        return ((group + 1 + t // per_group) % groups) * per_group + (t + sh // CORES) % per_group

    def fine_rows(p, t):
        return pl.ds(pl.multiple_of(p * half + pair(t) * share, share), share)

    def mass_row(at):
        tile = acc[at, width:]
        return jnp.broadcast_to(jnp.sum(jnp.where(eye, tile, 0.0), axis=0, keepdims=True), (8, 128))

    def part_copy(t):
        return pltpu.make_async_remote_copy(
            src_ref=part.at[t], dst_ref=other.at[t], send_sem=part_send.at[t], recv_sem=part_recv.at[t],
            device_id=partner, device_id_type=MESH,
        )

    mass_copy = pltpu.make_async_remote_copy(
        src_ref=mpart, dst_ref=mother, send_sem=mp_sem.at[0], recv_sem=mp_sem.at[1],
        device_id=partner, device_id_type=MESH,
    )

    def give(t, c):
        at = fine_rows(1 - core, t)
        part[t] = acc[at, :width].astype(BF16)
        part_copy(t).start()
        mpart[t] = mass_row(at)
        return c

    lax.fori_loop(0, halves, give, 0)
    mass_copy.start()
    add_last(core)

    def fin_copies(t):
        to = {"list": y * CORES + home, "shard": CORES * pair(t) + core}
        at = hidx * groups + group
        return [
            pltpu.make_async_remote_copy(
                src_ref=src.at[t], dst_ref=dst.at[at], send_sem=ss.at[t], recv_sem=rs.at[at],
                device_id=to, device_id_type=MESH,
            )
            for src, dst, ss, rs in ((merged, fin, fin_send, fin_recv), (mmerged, mfin, mf_send, mf_recv))
        ]

    def own_copies(t):
        at = hidx * groups + group
        return [
            pltpu.make_async_copy(merged.at[t], fin.at[at], fin_recv.at[at]),
            pltpu.make_async_copy(mmerged.at[t], mfin.at[at], mf_recv.at[at]),
        ]

    def is_own(t):
        return (home == core) & (CORES * pair(t) + core == sh)

    mass_copy.wait_recv()

    def forward(t, c):
        at = fine_rows(core, t)
        part_copy(t).wait_recv()
        merged[t] = (acc[at, :width] + other[t].astype(F32)).astype(BF16)
        mmerged[t] = mass_row(at) + mother[t]

        @pl.when(is_own(t))
        def _():
            for copy in own_copies(t):
                copy.start()

        @pl.when(jnp.logical_not(is_own(t)))
        def _():
            for copy in fin_copies(t):
                copy.start()

        return c

    lax.fori_loop(0, halves, forward, 0)

    @pl.when(core == home)
    def _():
        for copy in cent_far:
            copy.wait_send()

    def sent_parts(t, c):
        part_copy(t).wait_send()
        return c

    lax.fori_loop(0, halves, sent_parts, 0)
    mass_copy.wait_send()

    def arrived(i):
        return [
            pltpu.make_async_copy(fin.at[i], fin.at[i], fin_recv.at[i]),
            pltpu.make_async_copy(mfin.at[i], mfin.at[i], mf_recv.at[i]),
        ]

    own_in.wait()
    for h in range(local_lists):
        sums = own_s[h].astype(F32) * PRIOR
        mass = jnp.zeros((1, 128), F32)
        for k in range(groups):
            i = h * groups + k
            for copy in arrived(i):
                copy.wait()
            sums = sums + fin[i].astype(F32)
            mass = mass + mfin[i, 0:1, :]
        column = jnp.sum(jnp.where(eye, mass, 0.0), axis=1, keepdims=True)
        out_ref[h] = sums / (column + PRIOR)

    def sent_fin(t, c):
        @pl.when(jnp.logical_not(is_own(t)))
        def _():
            for copy in fin_copies(t):
                copy.wait_send()

        return c

    lax.fori_loop(0, halves, sent_fin, 0)


def solution(mesh):
    n_list, n_shard = mesh.shape["list"], mesh.shape["shard"]

    def per_device(embeddings, list_ids, centroids):
        rows, width = embeddings.shape
        local_lists, fine, _ = centroids.shape
        cap = rows // 8
        lists = local_lists * n_list
        full = lists * cap == rows
        sent = width if full else width + 128
        share = fine // n_shard
        halves = n_shard // CORES
        arrivals = local_lists * (n_shard // (local_lists * CORES))
        dma = pltpu.SemaphoreType.DMA
        vmem = pl.BlockSpec(memory_space=pltpu.VMEM)
        flops = 2 * rows * lists * cap * width + 4 * lists * cap * fine * width
        return pl.pallas_call(
            functools.partial(kernel, n_list, n_shard, full),
            out_shape=jax.ShapeDtypeStruct((local_lists, share, width), F32),
            in_specs=[vmem, pl.BlockSpec(memory_space=pl.ANY), pl.BlockSpec(memory_space=pl.ANY)],
            out_specs=vmem,
            scratch_shapes=[
                pltpu.VMEM((rows, width), BF16),
                pltpu.VMEM((local_lists, share, width), BF16),
                pltpu.VMEM((fine, cap), BF16),
                pltpu.VMEM((rows // cap, cap), F32),
                pltpu.VMEM((lists, cap, sent), BF16),
                pltpu.VMEM((lists, cap, sent), BF16),
                pltpu.VMEM((CORES, halves, share, width), BF16),
                pltpu.VMEM((fine, cap), F32),
                pltpu.VMEM((fine, width + 128), F32),
                pltpu.VMEM((halves, share, width), BF16),
                pltpu.VMEM((halves, 8, 128), F32),
                pltpu.VMEM((halves, share, width), BF16),
                pltpu.VMEM((halves, 8, 128), F32),
                pltpu.VMEM((halves, share, width), BF16),
                pltpu.VMEM((halves, 8, 128), F32),
                pltpu.VMEM((arrivals, share, width), BF16),
                pltpu.VMEM((arrivals, 8, 128), F32),
                dma((2,)),
                dma((3, CORES)),
                dma((lists,)),
                dma((lists,)),
                dma((halves,)),
                dma((halves,)),
                dma((2,)),
                dma((halves,)),
                dma((arrivals,)),
                dma((halves,)),
                dma((arrivals,)),
            ],
            compiler_params=pltpu.CompilerParams(
                collective_id=0, has_side_effects=True, vmem_limit_bytes=52 * 2**20
            ),
            cost_estimate=pl.CostEstimate(
                flops=flops, bytes_accessed=4 * rows * width, transcendentals=lists * cap * fine
            ),
        )(list_ids.T, embeddings, centroids.reshape(local_lists, halves, CORES, share, width))

    placed = (P(("list", "shard"), None), P(("list", "shard"), None), P("list", None, None))
    return jax.shard_map(
        per_device, mesh=mesh, in_specs=placed, out_specs=P("list", "shard", None), check_vma=False
    )
```
